32 devices in a mesh: group: 2 (over x), store: 4 (over z), tensor: 4 (over y, core).
Axes of the slice: x: 2, y: 2, z: 4, core: 2. Of those that a mesh axis runs over, the one named last changes fastest.
Arguments:
- queries: bfloat16 [2048, 8192], P(('group', 'store'), 'tensor'), parts along dimension 0, may hold values from -110 to 110
- cached_key_slabs: bfloat16 [2048, 8, 24, 128], P(('group', 'store'), 'tensor'), parts along dimension 0, may hold values from -6 to 6, as said below
- cached_value_slabs: bfloat16 [2048, 8, 24, 128], P(('group', 'store'), 'tensor'), parts along dimension 0, may hold values from -6 to 6, as said below
- request_cache_lengths: int32 [2048], P(('group', 'store')), parts along dimension 0, may hold values from 2 to 24, as said below
- output_projection_weight: bfloat16 [8192, 8192], P('tensor'), may hold values from -0.0625 to 0.0625
- adapter_shrink_weight: bfloat16 [32, 64, 8192], P('store', None, 'tensor'), may hold values from -0.0625 to 0.0625
- adapter_expand_weight: bfloat16 [32, 64, 8192], P('store', None, 'tensor'), may hold values from -0.75 to 0.75
- adapter_storage_slot: int32 [32], replicated, may hold values from 0 to 31, as said below
- wanted: int32 [4, 8], replicated, may hold values from 0 to 31, as said below
- request_wanted_entry: int32 [8, 256], P(('group', 'store')), parts along dimension 0, may hold values from 0 to 7, never falling along the last dimension, each value on 1 to 96 neighbouring positions
Outputs:
- mixed: bfloat16 [2048, 8192], P(('group', 'store'), 'tensor'), parts along dimension 0
The draws below stay inside these ranges and needn't reach their ends.
There are 2 independent parts, one for each index of `group`. The reference program is written for one: setup_inputs(seed, part) draws one part's arguments, and reference() takes and returns one part's arrays. A program takes and returns all parts, laid end to end along the dimension named above; an argument that names none is the same for every part. Nothing has to cross between parts.
Inputs may be any that keep to these rules, and one draw needn't show every extreme that they name: `cached_key_slabs`: slots s and t hold equal keys when s * 1 equals t * 1. `cached_value_slabs`: laid out as cached_key_slabs, with the same equal copies. `request_cache_lengths`: some request holds exactly 24 positions. A permutation: adapter a lies in slot adapter_storage_slot[a] of adapter_shrink_weight and adapter_expand_weight, held by store index adapter_storage_slot[a] // 8. `wanted`: each row names 8 different adapters; at most 2 of one row are held by one store index, and exactly 2 by some index in every row. `request_wanted_entry`: never falling along a row; every entry 0 to 7 is used by 1 to 96 requests of a row, one by exactly 96.
All inputs are finite; a program needn't handle non-finite values.
Results may differ from the reference program's by a relative error of at most 0.013.
Values may be sent and summed in bfloat16 or wider, within the bound.
No kernel may reach another device: no remote copies, remote signals or barrier semaphores. Data moves between devices by JAX's collectives and lax.ppermute only.
A program may use at most 384 MiB of HBM per device.

```python
import math
import jax
import jax.numpy as jnp
import numpy as np
from jax import lax

MODEL_WIDTH = 8192
HEADS = 64
KVH = 8
HD = 128
ADAPTER_RANK = 64
RQ = 256
L = 24
ADP_DEV = 8
USED_PER_STORE = 8
CAP = 2
MOST = 96
KV_SLOTS = 8
REQ = 1024
ADAPTER_TOTAL = 32
N_STORE = 4


def shared_keys(key):
    return jax.random.truncated_normal(key, -6.0, 6.0, (REQ, KVH, L, HD), jnp.float32)


def draw_cached_key_slabs(key, part):
    drawn = shared_keys(key)
    return jnp.repeat(drawn, KV_SLOTS // KVH, axis=1).astype(jnp.bfloat16)


def draw_cached_value_slabs(key, part):
    key = jax.random.fold_in(key, 9)
    drawn = jax.random.truncated_normal(key, -6.0, 6.0, (REQ, KVH, L, HD), jnp.float32)
    return jnp.repeat(drawn, KV_SLOTS // KVH, axis=1).astype(jnp.bfloat16)


def draw_queries(key, part):
    key = jax.random.fold_in(key, 7)
    drawn = jax.random.truncated_normal(key, -6.0, 6.0, (REQ, HEADS, HD), jnp.float32)
    return drawn.reshape(REQ, HEADS * HD).astype(jnp.bfloat16)


def draw_request_cache_lengths(key, part):
    key = jax.random.fold_in(key, 3)
    first_key, second_key = jax.random.split(key)
    lengths = jax.random.randint(first_key, (REQ,), 2, L + 1)
    longest = jax.random.randint(second_key, (), 0, REQ)
    return jnp.where(jnp.arange(REQ) == longest, L, lengths).astype(jnp.int32)


def routing(key):
    slot_of = jax.random.permutation(jax.random.fold_in(key, 101), ADAPTER_TOTAL).astype(jnp.int32)
    adapter_at = jnp.argsort(slot_of, stable=True).astype(jnp.int32)
    row_keys = jax.random.split(jax.random.fold_in(key, 102), N_STORE)

    def one_row(row_key):
        first_key, offset_key, order_key, shuffle_key = jax.random.split(row_key, 4)
        first_holder = jax.random.randint(first_key, (), 0, N_STORE)
        offsets = jax.random.randint(offset_key, (N_STORE,), 0, ADP_DEV)
        positions = jnp.arange(N_STORE * CAP)
        holder = positions // CAP
        within = positions % CAP
        candidate = holder * ADP_DEV + (within + offsets[holder]) % ADP_DEV
        score = jnp.where(holder == first_holder, within - CAP, jax.random.permutation(order_key, N_STORE * CAP))
        order = jnp.argsort(score, stable=True)
        picked = candidate[order[:USED_PER_STORE]]
        return picked[jax.random.permutation(shuffle_key, USED_PER_STORE)]
    slot_rows = jax.vmap(one_row)(row_keys)
    return (slot_of, adapter_at[slot_rows].astype(jnp.int32))


def draw_adapter_storage_slot(key, part):
    slot_of, chosen = routing(key)
    return slot_of


def draw_wanted(key, part):
    slot_of, chosen = routing(key)
    return chosen


def levels(own_key, extent, cuts, low, high):
    def one(axis_at, parts):
        draws = jax.random.uniform(jax.random.fold_in(jax.random.fold_in(own_key, 6), axis_at), (parts,), jnp.float32, low / len(cuts), high / len(cuts))
        return jnp.repeat(jnp.exp(draws), extent[axis_at] // parts).reshape((-1,) + (1,) * (len(extent) - axis_at - 1))

    loudness = one(*cuts[0])
    for cut in cuts[1:]:
        loudness = loudness * one(*cut)
    return loudness


def split_up(amount, total, bound, slope):
    weights = [(1 << 20) // math.isqrt(grade ** slope) + 1 for grade in range(2, amount + 1)]
    rest, holding = total - bound - (amount - 1), [1] * (amount - 1)
    while rest > 0:
        movable = [i for i in range(amount - 1) if holding[i] < bound]
        pool, left = sum([weights[i] for i in movable]), rest
        for i in movable:
            addition = min(bound - holding[i], max(1, left * weights[i] // pool), rest)
            holding[i] = holding[i] + addition
            rest = rest - addition
    return np.array([bound] + holding)


def ragged(own_key, amount, total, most, skew):
    if amount == 2:
        one = jax.random.randint(own_key, (), max(1, total - most), min(most, total - 1) + 1)
        return jnp.stack([one, total - one])
    sizes = jnp.asarray(split_up(amount, total, most, skew), jnp.int32)
    pairs = (amount - 1) // 2
    source_of, taker = sizes[1:1 + 2 * pairs:2], sizes[2:2 + 2 * pairs:2]
    margin = jnp.minimum(source_of - 1, most - taker)
    passed = jax.random.randint(jax.random.fold_in(own_key, 1), (pairs,), 0, 1 << 20) % (margin + 1)
    sizes = sizes.at[1:1 + 2 * pairs:2].set(source_of - passed).at[2:2 + 2 * pairs:2].set(taker + passed)
    return sizes[jax.random.permutation(jax.random.fold_in(own_key, 2), amount)]


def gaussian(own_key, dims, deviation, reach, cuts=(), held_as=jnp.bfloat16):
    values = deviation * jax.random.normal(own_key, dims, jnp.float32)
    if cuts:
        values = values * levels(own_key, dims, cuts, -0.22, 0.18)
    return jnp.clip(values, -reach, reach).astype(held_as)


def setup_inputs(seed: int = 0, part: int = 0) -> dict:
    key_list = jax.random.split(jax.random.key(seed), 11)
    part_keys = jax.random.split(jax.random.fold_in(key_list[10], part), 11)
    return {
        "queries": draw_queries(jax.random.fold_in(jax.random.fold_in(key_list[10], part), 71), part),
        "cached_key_slabs": draw_cached_key_slabs(jax.random.fold_in(jax.random.fold_in(key_list[10], part), 71), part),
        "cached_value_slabs": draw_cached_value_slabs(jax.random.fold_in(jax.random.fold_in(key_list[10], part), 71), part),
        "request_cache_lengths": draw_request_cache_lengths(jax.random.fold_in(jax.random.fold_in(key_list[10], part), 71), part),
        "output_projection_weight": gaussian(key_list[4], (MODEL_WIDTH, MODEL_WIDTH), MODEL_WIDTH ** -0.5, 0.0625, ((0, 4),)),
        "adapter_shrink_weight": gaussian(key_list[5], (ADAPTER_TOTAL, ADAPTER_RANK, MODEL_WIDTH), MODEL_WIDTH ** -0.5, 0.0625, ((0, 4), (2, 4))),
        "adapter_expand_weight": gaussian(key_list[6], (ADAPTER_TOTAL, ADAPTER_RANK, MODEL_WIDTH), ADAPTER_RANK ** -0.5, 0.75, ((0, 4), (2, 4))),
        "adapter_storage_slot": draw_adapter_storage_slot(jax.random.fold_in(key_list[10], 71), part),
        "wanted": draw_wanted(jax.random.fold_in(key_list[10], 71), part),
        "request_wanted_entry": jax.vmap(lambda own: jnp.searchsorted(jnp.cumsum(ragged(own, USED_PER_STORE, RQ, MOST, 2)), jnp.arange(RQ), side="right"))(jax.random.split(part_keys[9], N_STORE)).reshape((N_STORE, RQ)).astype(jnp.int32),
    }


def attend(queries, cached_key_slabs, cached_value_slabs, lengths):
    row_count = queries.shape[0]
    grouped = queries.astype(jnp.float32).reshape(row_count, KV_SLOTS, HEADS // KV_SLOTS, HD)
    scores = jnp.einsum('rsgd,rsld->rsgl', grouped, cached_key_slabs.astype(jnp.float32)) / math.sqrt(HD)
    visible = jnp.arange(L)[None, :] < lengths[:, None]
    scores = jnp.where(visible[:, None, None, :], scores, -jnp.inf)
    weights = jax.nn.softmax(scores, axis=-1).astype(jnp.bfloat16)
    attended = jnp.einsum('rsgl,rsld->rsgd', weights.astype(jnp.float32), cached_value_slabs.astype(jnp.float32))
    return attended.astype(jnp.bfloat16).reshape(row_count, MODEL_WIDTH)

def reference(queries, cached_key_slabs, cached_value_slabs, request_cache_lengths, output_projection_weight, adapter_shrink_weight, adapter_expand_weight, adapter_storage_slot, wanted, request_wanted_entry):
    slot_table = jnp.take(adapter_storage_slot, wanted, axis=0)

    def one_store(inputs):
        block_queries, block_keys, block_values, block_lengths, request_picks, slot_identifiers = inputs
        attended = attend(block_queries, block_keys, block_values, block_lengths)
        base_output = jnp.dot(attended, output_projection_weight, preferred_element_type=jnp.float32)
        shrink_rows = jnp.take(adapter_shrink_weight, slot_identifiers, axis=0).reshape(USED_PER_STORE * ADAPTER_RANK, MODEL_WIDTH)
        expand_rows = jnp.take(adapter_expand_weight, slot_identifiers, axis=0).reshape(USED_PER_STORE * ADAPTER_RANK, MODEL_WIDTH)
        selector = request_picks[:, None] == jnp.arange(USED_PER_STORE)[None, :]
        spread_in = jnp.dot(attended, shrink_rows.T, preferred_element_type=jnp.float32).reshape(RQ, USED_PER_STORE, ADAPTER_RANK)
        shrink = lax.optimization_barrier(jnp.sum(jnp.where(selector[:, :, None], spread_in, jnp.float32(0.0)), axis=1))
        shrink_low = shrink.astype(jnp.bfloat16)
        spread_across = jnp.where(selector[:, :, None], shrink_low[:, None, :], jnp.zeros((), jnp.bfloat16)).reshape(RQ, USED_PER_STORE * ADAPTER_RANK)
        adapter_delta = jnp.dot(spread_across, expand_rows, preferred_element_type=jnp.float32)
        return (base_output + adapter_delta).astype(jnp.bfloat16)
    stacked = (queries.reshape(N_STORE, RQ, MODEL_WIDTH), cached_key_slabs.reshape(N_STORE, RQ, KV_SLOTS, L, HD), cached_value_slabs.reshape(N_STORE, RQ, KV_SLOTS, L, HD), request_cache_lengths.reshape(N_STORE, RQ), request_wanted_entry, slot_table)
    mixed = lax.map(one_store, stacked)
    return mixed.reshape(REQ, MODEL_WIDTH)
```

```python
import functools
import math

import jax
import jax.numpy as jnp
from jax import lax
from jax.experimental import pallas as pl
from jax.experimental.pallas import tpu as pltpu
from jax.sharding import PartitionSpec as P

CAP = 2
ROWS = 8
MASKED = -1e30
MIB = 1 << 20
ANY = pl.BlockSpec(memory_space=pl.ANY)
HBM = pl.BlockSpec(memory_space=pltpu.HBM)
SMEM = pl.BlockSpec(memory_space=pltpu.SMEM)
VMEM = pl.BlockSpec(memory_space=pltpu.VMEM)


SMALL = pl.CostEstimate(flops=1, bytes_accessed=1, transcendentals=0)


def params(mib=56):
    return pltpu.CompilerParams(vmem_limit_bytes=mib * MIB)


def held_index(slots, wanted, row, holder, rank, per_store):
    index = jnp.int32(0)
    count = jnp.int32(0)
    for entry in range(wanted.shape[1]):
        local = slots[wanted[row, entry]] - holder * per_store
        held = jnp.logical_and(local >= 0, local < per_store)
        index = jnp.where(jnp.logical_and(held, count == rank), local, index)
        count = count + held.astype(jnp.int32)
    return index


def fetch_slabs(n_store, slots, wanted, source, held, sems):
    store, group = lax.axis_index("store"), lax.axis_index("group")
    per_store = source.shape[0]
    fetches = []
    for step in range(1, n_store):
        index = held_index(slots, wanted, lax.rem(store + step, n_store), store, group, per_store)
        fetch = pltpu.make_async_copy(source.at[index], held.at[step - 1], sems.at[step - 1])
        fetch.start()
        fetches.append(fetch)
    return fetches


def pass_slabs(fetches, held, outs, sems):
    copies = []
    for number, fetch in enumerate(fetches):
        fetch.wait()
        copy = pltpu.make_async_copy(held.at[number], outs[number], sems.at[number])
        copy.start()
        copies.append(copy)
    return copies


def pick_kernel(n_store, slots, wanted, source, *refs):
    outs, (info, held, in_sem, out_sem) = refs[: n_store - 1], refs[n_store - 1 :]
    store, group = lax.axis_index("store"), lax.axis_index("group")
    per_store = source.shape[0]
    fetches = fetch_slabs(n_store, slots, wanted, source, held, in_sem)
    for rank in range(CAP):
        info[rank] = held_index(slots, wanted, store, store, rank, per_store)
    used = wanted.shape[1]
    holders = [lax.div(slots[wanted[store, entry]], per_store) for entry in range(used)]
    for entry in range(used):
        rank = jnp.int32(0)
        for earlier in range(entry):
            rank = rank + (holders[earlier] == holders[entry]).astype(jnp.int32)
        step = lax.rem(store - holders[entry] + n_store, n_store)
        swapped = jnp.where(step == 0, rank, (rank != group).astype(jnp.int32))
        info[CAP + entry] = step * CAP + swapped
    for copy in pass_slabs(fetches, held, outs, out_sem):
        copy.wait()


def pick(slots, wanted, source):
    count = wanted.shape[0] - 1
    slab = jax.ShapeDtypeStruct(source.shape[1:], source.dtype)
    return pl.pallas_call(
        functools.partial(pick_kernel, count + 1),
        out_shape=[slab] * count + [jax.ShapeDtypeStruct((CAP + wanted.shape[1],), jnp.int32)],
        in_specs=[SMEM, SMEM, HBM],
        out_specs=[ANY] * count + [SMEM],
        scratch_shapes=[
            pltpu.VMEM((count,) + source.shape[1:], source.dtype),
            pltpu.SemaphoreType.DMA((count,)),
            pltpu.SemaphoreType.DMA((count,)),
        ],
        compiler_params=params(8),
        cost_estimate=SMALL,
        name="pick",
    )(slots, wanted, source)


def tie_kernel(*refs):
    pass


def tie(value, *earlier):
    return pl.pallas_call(
        tie_kernel,
        out_shape=jax.ShapeDtypeStruct(value.shape, value.dtype),
        in_specs=[ANY] * (1 + len(earlier)),
        out_specs=ANY,
        input_output_aliases={0: 0},
        compiler_params=params(2),
        cost_estimate=SMALL,
        name="tie",
    )(value, *earlier)


def attend_rows(first, count, lengths, q, k, v, out, slot_count, length, offset, row):
    heads = q.shape[1] // 128
    per_slot = heads // slot_count
    span = ROWS * slot_count * length
    scale = 1.0 / math.sqrt(128)
    finished = []
    for here in range(first, first + count, ROWS):
        limit = jnp.zeros((ROWS, span), jnp.int32)
        for r in range(ROWS):
            limit = jnp.where(row == r, lengths[here + r], limit)
        visible = jnp.logical_and(offset >= 0, offset < limit[None, None])
        rows = q[pl.ds(here // 16 * 16, 16), :].astype(jnp.float32)
        rows = rows[here % 16 : here % 16 + ROWS]
        stacked = jnp.concatenate(
            [rows[:, h * 128 : (h + 1) * 128] for h in range(heads)], axis=0
        ).astype(jnp.bfloat16)
        keys = k[pl.ds(here // ROWS * span, span), :]
        values = v[pl.ds(here // ROWS * span, span), :]
        scores = lax.dot_general(
            stacked, keys, (((1,), (1,)), ((), ())), preferred_element_type=jnp.float32
        ).reshape(slot_count, per_slot, ROWS, span)
        scores = jnp.where(visible, scores, MASKED)
        top = jnp.max(scores, axis=-1, keepdims=True)
        weights = jnp.exp((scores - top) * scale).reshape(heads * ROWS, span).astype(jnp.bfloat16)
        both = jnp.concatenate([values, jnp.ones_like(values)], axis=1)
        summed = jnp.dot(weights, both, preferred_element_type=jnp.float32)
        mean = summed[:, :128] / summed[:, 128:]
        finished.append(
            jnp.concatenate([mean[h * ROWS : (h + 1) * ROWS] for h in range(heads)], axis=1)
        )
        if len(finished) == 2:
            out[pl.ds(here - ROWS, 16), :] = jnp.concatenate(finished, axis=0).astype(out.dtype)
            finished = []


def weight_columns(step, n_chip, width, tile, weight, held, sems):
    tensor = lax.axis_index("tensor")
    chip = lax.rem(lax.div(tensor, 2) + step, n_chip)
    core = lax.rem(tensor, 2)
    fetches = []
    for number in range(2 * width // tile):
        block = chip * 2 + (1 - core if number * tile < width else core)
        start = pl.multiple_of(block * width + number * tile % width, tile)
        fetch = pltpu.make_async_copy(
            weight.at[:, pl.ds(start, tile)], held.at[number], sems.at[number]
        )
        fetch.start()
        fetches.append(fetch)
    return fetches


def project_rows(x, fetches, held, made, outs, sems):
    width, tile = made.shape[2], held.shape[2]
    steps = width // tile
    copies = []
    for block, pieces in enumerate(outs):
        for step in range(steps):
            fetches[block * steps + step].wait()
            total = jnp.dot(x[...], held[block * steps + step], preferred_element_type=jnp.float32)
            made[block, :, step * tile : (step + 1) * tile] = total.astype(made.dtype)
        size = made.shape[1] // len(pieces)
        for number, out in enumerate(pieces):
            copy = pltpu.make_async_copy(
                made.at[block, pl.ds(number * size, size)], out, sems.at[len(copies)]
            )
            copy.start()
            copies.append(copy)
    return copies


def front_kernel(n_store, n_chip, slot_count, length, chunk, slots, wanted, lengths, q_in, k_in, v_in, w_in, up_in, *refs):
    count = n_store - 1
    refs = refs[-(15 + count) :]
    refs[0][...] = jnp.zeros(refs[0].shape, refs[0].dtype)
    refs = refs[1:]
    attended, other, own = refs[:3]
    up_outs, refs = refs[3 : 3 + count], refs[3 + count :]
    qkv_sem, w_sem, up_sem, out_sem = refs[-4:]
    q, k, v, w, up = refs[:5]
    x, made = refs[5:7]
    rows, width = q.shape[0], made.shape[2]
    per_row = slot_count * length
    arrivals = []
    for part in range(rows // chunk):
        here = []
        for number, (source, held, size) in enumerate(
            ((q_in, q, chunk), (k_in, k, chunk * per_row), (v_in, v, chunk * per_row))
        ):
            span = pl.ds(part * size, size)
            fetch = pltpu.make_async_copy(source.at[span], held.at[span], qkv_sem.at[part, number])
            fetch.start()
            here.append(fetch)
        arrivals.append(here)
    columns = weight_columns(1, n_chip, width, w.shape[2], w_in, w, w_sem)
    slabs = fetch_slabs(n_store, slots, wanted, up_in, up, up_sem.at[0])
    span = ROWS * per_row
    shape = (slot_count, 1, ROWS, span)
    offset = (
        lax.broadcasted_iota(jnp.int32, shape, 3)
        - lax.broadcasted_iota(jnp.int32, shape, 2) * per_row
        - lax.broadcasted_iota(jnp.int32, shape, 0) * length
    )
    row = lax.broadcasted_iota(jnp.int32, (ROWS, span), 0)
    for part in range(rows // chunk):
        for fetch in arrivals[part]:
            fetch.wait()
        attend_rows(part * chunk, chunk, lengths, q, k, v, x, slot_count, length, offset, row)
    copies = [pltpu.make_async_copy(x, attended, out_sem.at[2])]
    copies[0].start()
    copies += pass_slabs(slabs, up, up_outs, up_sem.at[1])
    copies += project_rows(x, columns, w, made, ((other,), (own,)), out_sem)
    for copy in copies:
        copy.wait()


def front(n_chip, slots, wanted, lengths, queries, keys, values, weight, up, *earlier):
    rows, slot_count, length, head = keys.shape
    depth = queries.shape[1]
    count = wanted.shape[0] - 1
    width = up.shape[2]
    tile = min(512, width)
    tiles = 2 * width // tile
    chunk = min(64, rows)
    slab = jax.ShapeDtypeStruct(up.shape[1:], up.dtype)
    half = jax.ShapeDtypeStruct((rows, width), jnp.bfloat16)
    return pl.pallas_call(
        functools.partial(front_kernel, count + 1, n_chip, slot_count, length, chunk),
        out_shape=[jax.ShapeDtypeStruct((8, 128), jnp.float32)]
        + [jax.ShapeDtypeStruct((rows, depth), jnp.bfloat16), half, half]
        + [slab] * count,
        in_specs=[SMEM] * 3 + [HBM] * 5 + [SMEM] * len(earlier),
        out_specs=[VMEM] + [ANY] * (3 + count),
        scratch_shapes=[
            pltpu.VMEM((rows, depth), queries.dtype),
            pltpu.VMEM((rows * slot_count * length, head), keys.dtype),
            pltpu.VMEM((rows * slot_count * length, head), values.dtype),
            pltpu.VMEM((tiles, depth, tile), weight.dtype),
            pltpu.VMEM((count,) + up.shape[1:], up.dtype),
            pltpu.VMEM((rows, depth), jnp.bfloat16),
            pltpu.VMEM((2, rows, width), jnp.bfloat16),
            pltpu.SemaphoreType.DMA((rows // chunk, 3)),
            pltpu.SemaphoreType.DMA((tiles,)),
            pltpu.SemaphoreType.DMA((2, count)),
            pltpu.SemaphoreType.DMA((3,)),
        ],
        compiler_params=params(44),
        cost_estimate=SMALL,
        name="front",
    )(
        slots,
        wanted,
        lengths,
        queries,
        keys.reshape(-1, head),
        values.reshape(-1, head),
        weight,
        up,
        *earlier,
    )


def project_kernel(step, n_chip, pieces, x, w_in, *refs):
    refs = refs[-(5 + pieces) :]
    others, (own, w, made, w_sem, out_sem) = refs[:pieces], refs[pieces:]
    columns = weight_columns(step, n_chip, made.shape[2], w.shape[2], w_in, w, w_sem)
    for copy in project_rows(x, columns, w, made, (others, (own,)), out_sem):
        copy.wait()


def project(step, n_chip, pieces, attended, weight, width, *earlier):
    rows, depth = attended.shape
    tile = min(512, width)
    tiles = 2 * width // tile
    half = jax.ShapeDtypeStruct((rows, width), jnp.bfloat16)
    piece = jax.ShapeDtypeStruct((rows // pieces, width), jnp.bfloat16)
    return pl.pallas_call(
        functools.partial(project_kernel, step, n_chip, pieces),
        out_shape=[piece] * pieces + [half],
        in_specs=[VMEM, HBM] + [ANY] * len(earlier),
        out_specs=[ANY] * (pieces + 1),
        scratch_shapes=[
            pltpu.VMEM((tiles, depth, tile), weight.dtype),
            pltpu.VMEM((2, rows, width), jnp.bfloat16),
            pltpu.SemaphoreType.DMA((tiles,)),
            pltpu.SemaphoreType.DMA((pieces + 1,)),
        ],
        compiler_params=params(32),
        cost_estimate=SMALL,
        name="project",
    )(attended, weight, *earlier)


def place_row(info, entries):
    place = jnp.zeros(entries.shape, jnp.int32)
    for entry in range(info.shape[0] - CAP):
        place = jnp.where(entries == entry, info[CAP + entry], place)
    return place


def shrink_kernel(count, info, entries_ref, x_ref, near_ref, *refs):
    slab_refs, (o_ref, near, sem) = refs[:count], refs[-3:]
    fetches = []
    for rank in range(CAP):
        fetch = pltpu.make_async_copy(near_ref.at[info[rank]], near.at[rank], sem.at[rank])
        fetch.start()
        fetches.append(fetch)
    place = place_row(info, entries_ref[...])
    for fetch in fetches:
        fetch.wait()
    slabs = jnp.concatenate(
        [near[rank] for rank in range(CAP)] + [ref[...] for ref in slab_refs], axis=0
    )
    products = lax.dot_general(
        slabs, x_ref[...], (((1,), (1,)), ((), ())), preferred_element_type=jnp.float32
    )
    size = o_ref.shape[0]
    total = jnp.zeros(o_ref.shape, jnp.float32)
    for slot in range(slabs.shape[0] // size):
        total = total + jnp.where(place == slot, products[slot * size : (slot + 1) * size], 0.0)
    o_ref[...] = total


def shrink_part(info, entries, attended, near, slabs, *earlier):
    rows = attended.shape[0]
    _, size, width = near.shape
    return pl.pallas_call(
        functools.partial(shrink_kernel, len(slabs)),
        out_shape=jax.ShapeDtypeStruct((size, rows), jnp.float32),
        in_specs=[SMEM, VMEM, VMEM, HBM] + [VMEM] * len(slabs) + [ANY] * len(earlier),
        out_specs=VMEM,
        scratch_shapes=[
            pltpu.VMEM((CAP, size, width), near.dtype),
            pltpu.SemaphoreType.DMA((CAP,)),
        ],
        compiler_params=params(24),
        cost_estimate=SMALL,
        name="shrink",
    )(info, entries, attended, near, *slabs, *earlier)


def spread_kernel(slot_total, info, entries_ref, parts_ref, o_ref):
    place = place_row(info, entries_ref[...])
    low = jnp.sum(parts_ref[...], axis=0).astype(jnp.bfloat16).astype(jnp.float32)
    wide = jnp.concatenate(
        [jnp.where(place == slot, low, 0.0) for slot in range(slot_total)], axis=0
    )
    o_ref[...] = wide.T.astype(jnp.bfloat16)


def spread(info, entries, parts, slot_total):
    _, size, rows = parts.shape
    return pl.pallas_call(
        functools.partial(spread_kernel, slot_total),
        out_shape=jax.ShapeDtypeStruct((rows, slot_total * size), jnp.bfloat16),
        in_specs=[SMEM, VMEM, VMEM],
        out_specs=VMEM,
        compiler_params=params(12),
        cost_estimate=SMALL,
        name="spread",
    )(info, entries, parts)


def expand_kernel(count, part_count, info, wide_ref, near_ref, *refs):
    slab_refs, parts = refs[:count], refs[count : count + sum(part_count)]
    o_ref, near, sem = refs[-3:]
    fetches = []
    for rank in range(CAP):
        fetch = pltpu.make_async_copy(near_ref.at[info[rank]], near.at[rank], sem.at[rank])
        fetch.start()
        fetches.append(fetch)
    for fetch in fetches:
        fetch.wait()
    slabs = jnp.concatenate(
        [near[rank] for rank in range(CAP)] + [ref[...] for ref in slab_refs], axis=0
    )
    total = jnp.dot(wide_ref[...], slabs, preferred_element_type=jnp.float32)
    rest = iter(parts)
    for pieces in part_count:
        part = jnp.concatenate([next(rest)[...] for _ in range(pieces)], axis=0)
        total = total + part.astype(jnp.float32)
    o_ref[...] = total.astype(o_ref.dtype)


def expand(info, wide, near, slabs, parts):
    rows, width = parts[0][0].shape
    counts = [len(pieces) for pieces in parts]
    flat = [piece for pieces in parts for piece in pieces]
    return pl.pallas_call(
        functools.partial(expand_kernel, len(slabs), counts),
        out_shape=jax.ShapeDtypeStruct((rows, width), jnp.bfloat16),
        in_specs=[SMEM, VMEM, HBM] + [VMEM] * (len(slabs) + len(flat)),
        out_specs=VMEM,
        scratch_shapes=[
            pltpu.VMEM((CAP,) + near.shape[1:], near.dtype),
            pltpu.SemaphoreType.DMA((CAP,)),
        ],
        compiler_params=params(24),
        cost_estimate=SMALL,
        name="expand",
    )(info, wide, near, *slabs, *flat)


def shards(
    mesh,
    queries,
    cached_key_slabs,
    cached_value_slabs,
    request_cache_lengths,
    output_projection_weight,
    adapter_shrink_weight,
    adapter_expand_weight,
    adapter_storage_slot,
    wanted,
    request_wanted_entry,
):
    n_store, n_tensor = mesh.shape["store"], mesh.shape["tensor"]
    n_chip = n_tensor // 2
    local_width = adapter_shrink_weight.shape[2]
    far_steps = range(1, n_chip)

    def along_store(x, step):
        return lax.ppermute(x, "store", [(s, (s + step) % n_store) for s in range(n_store)])

    def swap_group(x):
        return lax.ppermute(x, "group", [(0, 1), (1, 0)])

    def swap_core(x):
        return lax.ppermute(x, "tensor", [(t, t ^ 1) for t in range(n_tensor)])

    def along_chip(x, step):
        return lax.ppermute(x, "tensor", [(t, (t + 2 * step) % n_tensor) for t in range(n_tensor)])

    slots = adapter_storage_slot
    *send_down, info = pick(slots, wanted, adapter_shrink_weight)
    got_down = [along_store(x, step + 1) for step, x in enumerate(send_down)]
    token, attended, other, own, *send_up = front(
        n_chip,
        slots,
        wanted,
        request_cache_lengths,
        queries,
        cached_key_slabs,
        cached_value_slabs,
        output_projection_weight,
        adapter_expand_weight,
        info,
    )
    got_down = [tie(x, token) for x in got_down[:2]] + got_down[2:]
    other = tie(other, *got_down[:2])

    def meet(mine, given):
        return (mine.astype(jnp.float32) + given.astype(jnp.float32)).astype(jnp.bfloat16)

    arrived = []
    for step in far_steps:
        if step > 1:
            other, own = project(step, n_chip, 1, attended, output_projection_weight, local_width, met)
        met = meet(own, swap_core(other))
        arrived.append([along_chip(met, step)])
    got_up = [along_store(tie(x, met), step + 1) for step, x in enumerate(send_up)]
    got_down = got_down[:2] + [tie(x, met) for x in got_down[2:]]
    *others, own = project(0, n_chip, 2, attended, output_projection_weight, local_width, met)
    near = [swap_core(x) for x in others]

    down = []
    for x in got_down:
        down += [x, swap_group(x)]
    part = shrink_part(info, request_wanted_entry, attended, adapter_shrink_weight, down, own)
    wide = spread(
        info, request_wanted_entry, lax.all_gather(part, "tensor"), n_store * CAP
    )
    up = []
    for x, earlier in zip(got_up, [own, part, wide] + [wide] * n_store):
        x = tie(x, earlier)
        up += [x, swap_group(x)]
    return expand(info, wide, adapter_expand_weight, up, [[own], near] + arrived)


def solution(mesh):
    placed = (
        P(("group", "store"), "tensor"),
        P(("group", "store"), "tensor", None, None),
        P(("group", "store"), "tensor", None, None),
        P(("group", "store")),
        P("tensor", None),
        P("store", None, "tensor"),
        P("store", None, "tensor"),
        P(),
        P(),
        P(("group", "store"), None),
    )
    return jax.shard_map(
        functools.partial(shards, mesh),
        mesh=mesh,
        in_specs=placed,
        out_specs=P(("group", "store"), "tensor"),
        check_vma=False,
    )
```

```python
import functools
import math

import jax
import jax.numpy as jnp
from jax import lax
from jax.experimental import pallas as pl
from jax.experimental.pallas import tpu as pltpu
from jax.sharding import PartitionSpec as P

CAP = 2
ROWS = 8
MASKED = -1e30
AHEAD = 4
CHUNK = 32
MIB = 1 << 20
ANY = pl.BlockSpec(memory_space=pl.ANY)
HBM = pl.BlockSpec(memory_space=pltpu.HBM)
SMEM = pl.BlockSpec(memory_space=pltpu.SMEM)
VMEM = pl.BlockSpec(memory_space=pltpu.VMEM)


SMALL = pl.CostEstimate(flops=1, bytes_accessed=1, transcendentals=0)


def params(mib=56):
    return pltpu.CompilerParams(vmem_limit_bytes=mib * MIB)


def held_index(slots, wanted, row, holder, rank, per_store):
    index = jnp.int32(0)
    count = jnp.int32(0)
    for entry in range(wanted.shape[1]):
        local = slots[wanted[row, entry]] - holder * per_store
        held = jnp.logical_and(local >= 0, local < per_store)
        index = jnp.where(jnp.logical_and(held, count == rank), local, index)
        count = count + held.astype(jnp.int32)
    return index


def pick_kernel(n_store, slots_in, wanted_in, down, up, *refs):
    targets, (info, slots, wanted, held, table_sem, in_sem, out_sem) = refs[:-7], refs[-7:]
    tables = [
        pltpu.make_async_copy(slots_in, slots, table_sem.at[0]),
        pltpu.make_async_copy(wanted_in, wanted, table_sem.at[1]),
    ]
    for table in tables:
        table.start()
    for table in tables:
        table.wait()
    store, group = lax.axis_index("store"), lax.axis_index("group")
    per_store = down.shape[0]
    indices = [
        held_index(slots, wanted, store ^ step, store, group, per_store)
        for step in range(CAP, n_store)
    ]
    indices += [
        held_index(slots, wanted, store ^ 1, store, rank, per_store) for rank in range(CAP)
    ]
    count = len(indices)
    targets = (
        list(targets[:count])
        + list(targets[count:-1])
        + [targets[-1].at[rank] for rank in range(CAP)]
    )
    fetches = []
    for source in (down, up):
        for index in indices:
            slot = len(fetches)
            fetch = pltpu.make_async_copy(source.at[index], held.at[slot], in_sem.at[slot])
            fetch.start()
            fetches.append(fetch)
    for rank in range(CAP):
        info[rank] = held_index(slots, wanted, store, store, rank, per_store)
    used = wanted.shape[1]
    holders = [lax.div(slots[wanted[store, entry]], per_store) for entry in range(used)]
    for entry in range(used):
        rank = jnp.int32(0)
        for earlier in range(entry):
            rank = rank + (holders[earlier] == holders[entry]).astype(jnp.int32)
        step = store ^ holders[entry]
        far = CAP + step + jnp.where(rank == group, 0, n_store - CAP)
        info[CAP + entry] = jnp.where(step <= 1, step * CAP + rank, far)
    copies = []
    for slot, target in enumerate(targets):
        fetches[slot].wait()
        copies.append(pltpu.make_async_copy(held.at[slot], target, out_sem.at[slot]))
        copies[-1].start()
    for copy in copies:
        copy.wait()


def pick(slots, wanted, down, up):
    n_store = wanted.shape[0]
    slab = jax.ShapeDtypeStruct(down.shape[1:], down.dtype)
    pair = jax.ShapeDtypeStruct((CAP,) + down.shape[1:], down.dtype)
    outs = [slab] * n_store + [slab] * (n_store - CAP) + [pair]
    return pl.pallas_call(
        functools.partial(pick_kernel, n_store),
        out_shape=outs + [jax.ShapeDtypeStruct((CAP + wanted.shape[1],), jnp.int32)],
        in_specs=[ANY, ANY, HBM, HBM],
        out_specs=[ANY] * len(outs) + [SMEM],
        scratch_shapes=[
            pltpu.SMEM(slots.shape, slots.dtype),
            pltpu.SMEM(wanted.shape, wanted.dtype),
            pltpu.VMEM((2 * n_store,) + down.shape[1:], down.dtype),
            pltpu.SemaphoreType.DMA((2,)),
            pltpu.SemaphoreType.DMA((2 * n_store,)),
            pltpu.SemaphoreType.DMA((2 * n_store,)),
        ],
        compiler_params=params(60),
        cost_estimate=SMALL,
        name="pick",
    )(slots, wanted, down, up)


def stack_kernel(count, *refs):
    o_ref = refs[-1]
    for number in range(count):
        o_ref[number] = refs[number][...]


def stack(slabs, *earlier):
    return pl.pallas_call(
        functools.partial(stack_kernel, len(slabs)),
        out_shape=jax.ShapeDtypeStruct((len(slabs),) + slabs[0].shape, slabs[0].dtype),
        in_specs=[VMEM] * len(slabs) + [ANY] * len(earlier),
        out_specs=VMEM,
        compiler_params=params(8),
        cost_estimate=SMALL,
        name="stack",
    )(*slabs, *earlier)


def tie_kernel(*refs):
    pass


def tie(value, *earlier):
    return pl.pallas_call(
        tie_kernel,
        out_shape=jax.ShapeDtypeStruct(value.shape, value.dtype),
        in_specs=[ANY] * (1 + len(earlier)),
        out_specs=ANY,
        input_output_aliases={0: 0},
        compiler_params=params(2),
        cost_estimate=SMALL,
        name="tie",
    )(value, *earlier)


def attend_rows(first, count, lengths, q, k, v, out, slot_count, length, offset, row):
    heads = q.shape[1] // 128
    per_slot = heads // slot_count
    span = ROWS * slot_count * length
    scale = 1.0 / math.sqrt(128)
    finished = []
    for here in range(first, first + count, ROWS):
        limit = jnp.zeros((ROWS, span), jnp.int32)
        for r in range(ROWS):
            limit = jnp.where(row == r, lengths[here + r], limit)
        visible = jnp.logical_and(offset >= 0, offset < limit[None, None])
        rows = q[pl.ds(here // 16 * 16, 16), :].astype(jnp.float32)
        rows = rows[here % 16 : here % 16 + ROWS]
        stacked = jnp.concatenate(
            [rows[:, h * 128 : (h + 1) * 128] for h in range(heads)], axis=0
        ).astype(jnp.bfloat16)
        keys = k[pl.ds(here // ROWS * span, span), :]
        values = v[pl.ds(here // ROWS * span, span), :]
        scores = lax.dot_general(
            stacked, keys, (((1,), (1,)), ((), ())), preferred_element_type=jnp.float32
        ).reshape(slot_count, per_slot, ROWS, span)
        scores = jnp.where(visible, scores, MASKED)
        top = jnp.max(scores, axis=-1, keepdims=True)
        weights = jnp.exp((scores - top) * scale).reshape(heads * ROWS, span).astype(jnp.bfloat16)
        both = jnp.concatenate([values, jnp.ones_like(values)], axis=1)
        summed = jnp.dot(weights, both, preferred_element_type=jnp.float32)
        mean = summed[:, :128] / summed[:, 128:]
        finished.append(
            jnp.concatenate([mean[h * ROWS : (h + 1) * ROWS] for h in range(heads)], axis=1)
        )
        if len(finished) == 2:
            out[pl.ds(here - ROWS, 16), :] = jnp.concatenate(finished, axis=0).astype(out.dtype)
            finished = []


class Stream:
    def __init__(self, jobs, ahead):
        self.jobs, self.ahead, self.next = jobs, ahead, 0
        for job in jobs[:ahead]:
            self.start(job)

    def start(self, job):
        for copy in job:
            copy.start()

    def take(self):
        for copy in self.jobs[self.next]:
            copy.wait()
        for job in self.jobs[self.next + self.ahead : self.next + self.ahead + 1]:
            self.start(job)
        self.next += 1


def weight_columns(step, n_chip, width, tile, weight, held, sems):
    tensor = lax.axis_index("tensor")
    chip = lax.rem(lax.div(tensor, 2) + step, n_chip)
    core = lax.rem(tensor, 2)
    jobs = []
    for number in range(2 * width // tile):
        block = chip * 2 + (1 - core if number * tile < width else core)
        start = pl.multiple_of(block * width + number * tile % width, tile)
        jobs.append(
            [
                pltpu.make_async_copy(
                    weight.at[:, pl.ds(start, tile)], held.at[number], sems.at[number]
                )
            ]
        )
    return jobs


def project_rows(x, stream, held, made, outs, sems):
    width, tile = made.shape[2], held.shape[2]
    steps = width // tile
    copies = []
    for block, out in enumerate(outs):
        for step in range(steps):
            stream.take()
            total = jnp.dot(x[...], held[block * steps + step], preferred_element_type=jnp.float32)
            made[block, :, step * tile : (step + 1) * tile] = total.astype(made.dtype)
        copy = pltpu.make_async_copy(made.at[block], out, sems.at[block])
        copy.start()
        copies.append(copy)
    return copies


def front_kernel(n_chip, slot_count, length, chunk, lengths_in, q_in, k_in, v_in, w_in, *refs):
    flag, attended, other, own = refs[-15:-11]
    lengths, q, k, v, w, x, made, lengths_sem, qkv_sem, w_sem, out_sem = refs[-11:]
    rows, width = q.shape[0], made.shape[2]
    per_row = slot_count * length
    jobs = []
    for part in range(rows // chunk):
        job = []
        for number, (source, held, size) in enumerate(
            ((q_in, q, chunk), (k_in, k, chunk * per_row), (v_in, v, chunk * per_row))
        ):
            span = pl.ds(part * size, size)
            job.append(
                pltpu.make_async_copy(source.at[span], held.at[span], qkv_sem.at[part, number])
            )
        jobs.append(job)
    jobs[0].append(pltpu.make_async_copy(lengths_in, lengths, lengths_sem.at[0]))
    stream = Stream(
        jobs + weight_columns(1, n_chip, width, w.shape[2], w_in, w, w_sem), AHEAD
    )
    span = ROWS * per_row
    shape = (slot_count, 1, ROWS, span)
    offset = (
        lax.broadcasted_iota(jnp.int32, shape, 3)
        - lax.broadcasted_iota(jnp.int32, shape, 2) * per_row
        - lax.broadcasted_iota(jnp.int32, shape, 0) * length
    )
    row = lax.broadcasted_iota(jnp.int32, (ROWS, span), 0)
    for part in range(rows // chunk):
        stream.take()
        attend_rows(part * chunk, chunk, lengths, q, k, v, x, slot_count, length, offset, row)
    flag[0] = lengths[0]
    copies = [pltpu.make_async_copy(x, attended, out_sem.at[2])]
    copies[0].start()
    copies += project_rows(x, stream, w, made, (other, own), out_sem)
    for copy in copies:
        copy.wait()


def front(n_chip, lengths, queries, keys, values, weight, width, *earlier):
    rows, slot_count, length, head = keys.shape
    depth = queries.shape[1]
    tile = min(512, width)
    tiles = 2 * width // tile
    chunk = min(CHUNK, rows)
    half = jax.ShapeDtypeStruct((rows, width), jnp.bfloat16)
    return pl.pallas_call(
        functools.partial(front_kernel, n_chip, slot_count, length, chunk),
        out_shape=[
            jax.ShapeDtypeStruct((1,), jnp.int32),
            jax.ShapeDtypeStruct((rows, depth), jnp.bfloat16),
            half,
            half,
        ],
        in_specs=[ANY] + [HBM] * 4 + [ANY] * len(earlier),
        out_specs=[SMEM] + [ANY] * 3,
        scratch_shapes=[
            pltpu.SMEM(lengths.shape, lengths.dtype),
            pltpu.VMEM((rows, depth), queries.dtype),
            pltpu.VMEM((rows * slot_count * length, head), keys.dtype),
            pltpu.VMEM((rows * slot_count * length, head), values.dtype),
            pltpu.VMEM((tiles, depth, tile), weight.dtype),
            pltpu.VMEM((rows, depth), jnp.bfloat16),
            pltpu.VMEM((2, rows, width), jnp.bfloat16),
            pltpu.SemaphoreType.DMA((1,)),
            pltpu.SemaphoreType.DMA((rows // chunk, 3)),
            pltpu.SemaphoreType.DMA((tiles,)),
            pltpu.SemaphoreType.DMA((3,)),
        ],
        compiler_params=params(58),
        cost_estimate=SMALL,
        name="front",
    )(
        lengths,
        queries,
        keys.reshape(-1, head),
        values.reshape(-1, head),
        weight,
        *earlier,
    )


def project_kernel(step, n_chip, x, w_in, *refs):
    other, own, w, made, w_sem, out_sem = refs[-6:]
    stream = Stream(
        weight_columns(step, n_chip, made.shape[2], w.shape[2], w_in, w, w_sem), AHEAD
    )
    for copy in project_rows(x, stream, w, made, (other, own), out_sem):
        copy.wait()


def project(step, n_chip, attended, weight, width, *earlier):
    rows, depth = attended.shape
    tile = min(512, width)
    tiles = 2 * width // tile
    half = jax.ShapeDtypeStruct((rows, width), jnp.bfloat16)
    return pl.pallas_call(
        functools.partial(project_kernel, step, n_chip),
        out_shape=[half, half],
        in_specs=[VMEM, HBM] + [ANY] * len(earlier),
        out_specs=[ANY] * 2,
        scratch_shapes=[
            pltpu.VMEM((tiles, depth, tile), weight.dtype),
            pltpu.VMEM((2, rows, width), jnp.bfloat16),
            pltpu.SemaphoreType.DMA((tiles,)),
            pltpu.SemaphoreType.DMA((2,)),
        ],
        compiler_params=params(32),
        cost_estimate=SMALL,
        name="project",
    )(attended, weight, *earlier)


def place_row(info, entries):
    place = jnp.zeros(entries.shape, jnp.int32)
    for entry in range(info.shape[0] - CAP):
        place = jnp.where(entries == entry, info[CAP + entry], place)
    return place


def shrink_kernel(count, info, entries_ref, x_ref, near_ref, *refs):
    slab_refs, (o_ref, near, sem) = refs[:count], refs[-3:]
    fetches = []
    for rank in range(CAP):
        fetch = pltpu.make_async_copy(near_ref.at[info[rank]], near.at[rank], sem.at[rank])
        fetch.start()
        fetches.append(fetch)
    place = place_row(info, entries_ref[...])
    for fetch in fetches:
        fetch.wait()
    slabs = jnp.concatenate(
        [near[rank] for rank in range(CAP)]
        + [ref[...].reshape(-1, ref.shape[-1]) for ref in slab_refs],
        axis=0,
    )
    products = lax.dot_general(
        slabs, x_ref[...], (((1,), (1,)), ((), ())), preferred_element_type=jnp.float32
    )
    size = o_ref.shape[0]
    total = jnp.zeros(o_ref.shape, jnp.float32)
    for slot in range(slabs.shape[0] // size):
        total = total + jnp.where(place == slot, products[slot * size : (slot + 1) * size], 0.0)
    o_ref[...] = total


def shrink_part(info, entries, attended, near, slabs, *earlier):
    rows = attended.shape[0]
    _, size, width = near.shape
    return pl.pallas_call(
        functools.partial(shrink_kernel, len(slabs)),
        out_shape=jax.ShapeDtypeStruct((size, rows), jnp.float32),
        in_specs=[SMEM, VMEM, VMEM, HBM] + [VMEM] * len(slabs) + [ANY] * len(earlier),
        out_specs=VMEM,
        scratch_shapes=[
            pltpu.VMEM((CAP, size, width), near.dtype),
            pltpu.SemaphoreType.DMA((CAP,)),
        ],
        compiler_params=params(24),
        cost_estimate=SMALL,
        name="shrink",
    )(info, entries, attended, near, *slabs, *earlier)


def spread_kernel(slot_total, info, entries_ref, parts_ref, *refs):
    o_ref = refs[-1]
    place = place_row(info, entries_ref[...])
    low = jnp.sum(parts_ref[...], axis=0).astype(jnp.bfloat16).astype(jnp.float32)
    wide = jnp.concatenate(
        [jnp.where(place == slot, low, 0.0) for slot in range(slot_total)], axis=0
    )
    o_ref[...] = wide.T.astype(jnp.bfloat16)


def spread(info, entries, parts, slot_total, *earlier):
    _, size, rows = parts.shape
    return pl.pallas_call(
        functools.partial(spread_kernel, slot_total),
        out_shape=jax.ShapeDtypeStruct((rows, slot_total * size), jnp.bfloat16),
        in_specs=[SMEM, VMEM, VMEM] + [ANY] * len(earlier),
        out_specs=VMEM,
        compiler_params=params(12),
        cost_estimate=SMALL,
        name="spread",
    )(info, entries, parts, *earlier)


def expand_kernel(count, part_count, info, wide_ref, near_ref, *refs):
    slab_refs, parts = refs[:count], refs[count : count + sum(part_count)]
    o_ref, near, sem = refs[-3:]
    fetches = []
    for rank in range(CAP):
        fetch = pltpu.make_async_copy(near_ref.at[info[rank]], near.at[rank], sem.at[rank])
        fetch.start()
        fetches.append(fetch)
    for fetch in fetches:
        fetch.wait()
    slabs = jnp.concatenate(
        [near[rank] for rank in range(CAP)]
        + [ref[...].reshape(-1, ref.shape[-1]) for ref in slab_refs],
        axis=0,
    )
    total = jnp.dot(
        wide_ref[:, : slabs.shape[0]], slabs, preferred_element_type=jnp.float32
    )
    rest = iter(parts)
    for pieces in part_count:
        part = jnp.concatenate([next(rest)[...] for _ in range(pieces)], axis=0)
        total = total + part.astype(jnp.float32)
    o_ref[...] = total.astype(o_ref.dtype)


def expand(info, wide, near, slabs, parts, *earlier):
    rows, width = parts[0][0].shape
    counts = [len(pieces) for pieces in parts]
    flat = [piece for pieces in parts for piece in pieces]
    return pl.pallas_call(
        functools.partial(expand_kernel, len(slabs), counts),
        out_shape=jax.ShapeDtypeStruct((rows, width), jnp.float32),
        in_specs=[SMEM, VMEM, HBM] + [VMEM] * (len(slabs) + len(flat)) + [ANY] * len(earlier),
        out_specs=VMEM,
        scratch_shapes=[
            pltpu.VMEM((CAP,) + near.shape[1:], near.dtype),
            pltpu.SemaphoreType.DMA((CAP,)),
        ],
        compiler_params=params(24),
        cost_estimate=SMALL,
        name="expand",
    )(info, wide, near, *slabs, *flat, *earlier)


def finish_kernel(wide_ref, total_ref, *refs):
    slab_refs, o_ref = refs[:-1], refs[-1]
    slabs = jnp.concatenate([ref[...] for ref in slab_refs], axis=0)
    first = wide_ref.shape[1] - slabs.shape[0]
    delta = jnp.dot(wide_ref[:, first:], slabs, preferred_element_type=jnp.float32)
    o_ref[...] = (total_ref[...] + delta).astype(o_ref.dtype)


def finish(wide, total, slabs):
    return pl.pallas_call(
        finish_kernel,
        out_shape=jax.ShapeDtypeStruct(total.shape, jnp.bfloat16),
        in_specs=[VMEM] * (2 + len(slabs)),
        out_specs=VMEM,
        compiler_params=params(24),
        cost_estimate=SMALL,
        name="finish",
    )(wide, total, *slabs)


def shards(
    mesh,
    queries,
    cached_key_slabs,
    cached_value_slabs,
    request_cache_lengths,
    output_projection_weight,
    adapter_shrink_weight,
    adapter_expand_weight,
    adapter_storage_slot,
    wanted,
    request_wanted_entry,
):
    n_store, n_tensor = mesh.shape["store"], mesh.shape["tensor"]
    n_chip = n_tensor // 2
    local_width = adapter_shrink_weight.shape[2]
    far_steps = range(1, n_chip)

    def along_store(x, step):
        return lax.ppermute(x, "store", [(s, s ^ step) for s in range(n_store)])

    def swap_group(x):
        return lax.ppermute(x, "group", [(0, 1), (1, 0)])

    def swap_core(x):
        return lax.ppermute(x, "tensor", [(t, t ^ 1) for t in range(n_tensor)])

    def along_chip(x, step):
        return lax.ppermute(x, "tensor", [(t, (t + 2 * step) % n_tensor) for t in range(n_tensor)])

    weight = output_projection_weight
    *picked, send_pair, info = pick(
        adapter_storage_slot, wanted, adapter_shrink_weight, adapter_expand_weight
    )
    steps = range(CAP, n_store)
    own_down = [along_store(x, step) for step, x in zip(steps, picked)]
    next_down = [along_store(x, 1) for x in picked[len(steps) : n_store]]
    send_up = picked[n_store:]
    flag, attended, other, own = front(
        n_chip,
        request_cache_lengths,
        queries,
        cached_key_slabs,
        cached_value_slabs,
        weight,
        local_width,
        info,
    )

    def meet(mine, given):
        return (mine.astype(jnp.float32) + given.astype(jnp.float32)).astype(jnp.bfloat16)

    def join(other, own):
        return lax.cond(
            flag[0] > 0,
            lambda: meet(own, swap_core(other)),
            lambda: meet(swap_core(other), own),
        )

    arrived = []
    for step in far_steps:
        if step > 1:
            other, own = project(step, n_chip, attended, weight, local_width, met)
        met = join(other, own)
        arrived.append([along_chip(met, step)])
    own_up = [along_store(tie(x, met), step) for step, x in zip(steps, send_up)]
    next_up = along_store(tie(send_pair, met), 1)
    own_down = stack(own_down, met, *next_down)
    swapped_down = swap_group(own_down)
    other, own = project(0, n_chip, attended, weight, local_width, met)

    def middle(first):
        given = swap_core(other)
        swapped = [swap_group(x) for x in own_up[:-1]]
        part = shrink_part(
            info,
            request_wanted_entry,
            attended,
            adapter_shrink_weight,
            [*next_down, own_down, swapped_down],
        )
        base = meet(own, given) if first else meet(given, own)
        return base, swapped, lax.all_gather(part, "tensor")

    base, swapped_up, gathered = lax.cond(
        flag[0] > 0, lambda: middle(True), lambda: middle(False)
    )
    wide = spread(info, request_wanted_entry, gathered, n_store * CAP)
    last = tie(own_up[-1], wide)
    swapped = swap_group(last)
    total = expand(
        info,
        wide,
        adapter_expand_weight,
        [next_up] + own_up[:-1] + [last] + swapped_up,
        [[base]] + arrived,
    )
    return finish(wide, total, [swapped])


def solution(mesh):
    placed = (
        P(("group", "store"), "tensor"),
        P(("group", "store"), "tensor", None, None),
        P(("group", "store"), "tensor", None, None),
        P(("group", "store")),
        P("tensor", None),
        P("store", None, "tensor"),
        P("store", None, "tensor"),
        P(),
        P(),
        P(("group", "store"), None),
    )
    return jax.shard_map(
        functools.partial(shards, mesh),
        mesh=mesh,
        in_specs=placed,
        out_specs=P(("group", "store"), "tensor"),
        check_vma=False,
    )
```

```python
import functools
import math

import jax
import jax.numpy as jnp
from jax import lax
from jax.experimental import pallas as pl
from jax.experimental.pallas import tpu as pltpu
from jax.sharding import PartitionSpec as P

CAP = 2
ROWS = 8
MASKED = -1e30
AHEAD = 4
CHUNK = 64
MIB = 1 << 20
ANY = pl.BlockSpec(memory_space=pl.ANY)
HBM = pl.BlockSpec(memory_space=pltpu.HBM)
SMEM = pl.BlockSpec(memory_space=pltpu.SMEM)
VMEM = pl.BlockSpec(memory_space=pltpu.VMEM)


SMALL = pl.CostEstimate(flops=1, bytes_accessed=1, transcendentals=0)


def params(mib=56):
    return pltpu.CompilerParams(vmem_limit_bytes=mib * MIB)


def held_index(slots, wanted, row, holder, rank, per_store):
    index = jnp.int32(0)
    count = jnp.int32(0)
    for entry in range(wanted.shape[1]):
        local = slots[wanted[row, entry]] - holder * per_store
        held = jnp.logical_and(local >= 0, local < per_store)
        index = jnp.where(jnp.logical_and(held, count == rank), local, index)
        count = count + held.astype(jnp.int32)
    return index


def pick_kernel(n_store, slots_in, wanted_in, down, *refs):
    outs, (info, sends, slots, wanted, held, table_sem, in_sem, out_sem) = refs[:-8], refs[-8:]
    tables = [
        pltpu.make_async_copy(slots_in, slots, table_sem.at[0]),
        pltpu.make_async_copy(wanted_in, wanted, table_sem.at[1]),
    ]
    for table in tables:
        table.start()
    for table in tables:
        table.wait()
    store, group = lax.axis_index("store"), lax.axis_index("group")
    per_store = down.shape[0]
    indices = [
        held_index(slots, wanted, store ^ step, store, group, per_store)
        for step in range(CAP, n_store)
    ]
    indices += [
        held_index(slots, wanted, store ^ 1, store, rank, per_store) for rank in range(CAP)
    ]
    fetches = []
    for slot, index in enumerate(indices):
        fetch = pltpu.make_async_copy(down.at[index], held.at[slot], in_sem.at[slot])
        fetch.start()
        fetches.append(fetch)
        sends[slot] = index
    for rank in range(CAP):
        info[rank] = held_index(slots, wanted, store, store, rank, per_store)
    used = wanted.shape[1]
    holders = [lax.div(slots[wanted[store, entry]], per_store) for entry in range(used)]
    for entry in range(used):
        rank = jnp.int32(0)
        for earlier in range(entry):
            rank = rank + (holders[earlier] == holders[entry]).astype(jnp.int32)
        step = store ^ holders[entry]
        far = CAP + step + jnp.where(rank == group, 0, n_store - CAP)
        info[CAP + entry] = jnp.where(step <= 1, step * CAP + rank, far)
    copies = []
    for slot, target in enumerate(outs):
        fetches[slot].wait()
        copies.append(pltpu.make_async_copy(held.at[slot], target, out_sem.at[slot]))
        copies[-1].start()
    for copy in copies:
        copy.wait()


def pick(slots, wanted, down):
    n_store = wanted.shape[0]
    slab = jax.ShapeDtypeStruct(down.shape[1:], down.dtype)
    return pl.pallas_call(
        functools.partial(pick_kernel, n_store),
        out_shape=[slab] * n_store
        + [
            jax.ShapeDtypeStruct((CAP + wanted.shape[1],), jnp.int32),
            jax.ShapeDtypeStruct((n_store,), jnp.int32),
        ],
        in_specs=[ANY, ANY, HBM],
        out_specs=[ANY] * n_store + [SMEM, SMEM],
        scratch_shapes=[
            pltpu.SMEM(slots.shape, slots.dtype),
            pltpu.SMEM(wanted.shape, wanted.dtype),
            pltpu.VMEM((n_store,) + down.shape[1:], down.dtype),
            pltpu.SemaphoreType.DMA((2,)),
            pltpu.SemaphoreType.DMA((n_store,)),
            pltpu.SemaphoreType.DMA((n_store,)),
        ],
        compiler_params=params(62),
        cost_estimate=SMALL,
        name="pick",
    )(slots, wanted, down)


def stack_kernel(count, *refs):
    o_ref = refs[-1]
    slabs = refs[-1 - count : -1]
    for number in range(count):
        o_ref[number] = slabs[number][...]


def stack(slabs, *earlier):
    return pl.pallas_call(
        functools.partial(stack_kernel, len(slabs)),
        out_shape=jax.ShapeDtypeStruct((len(slabs),) + slabs[0].shape, slabs[0].dtype),
        in_specs=[ANY] * len(earlier) + [VMEM] * len(slabs),
        out_specs=VMEM,
        compiler_params=params(8),
        cost_estimate=SMALL,
        name="stack",
    )(*earlier, *slabs)


def tie_kernel(*refs):
    pass


def tie(value, *earlier):
    return pl.pallas_call(
        tie_kernel,
        out_shape=jax.ShapeDtypeStruct(value.shape, value.dtype),
        in_specs=[ANY] * (1 + len(earlier)),
        out_specs=ANY,
        input_output_aliases={0: 0},
        compiler_params=params(2),
        cost_estimate=SMALL,
        name="tie",
    )(value, *earlier)


def attend_rows(first, count, lengths, q, k, v, out, slot_count, length, offset, row):
    heads = q.shape[1] // 128
    per_slot = heads // slot_count
    span = ROWS * slot_count * length
    scale = 1.0 / math.sqrt(128)
    finished = []
    for here in range(first, first + count, ROWS):
        limit = jnp.zeros((ROWS, span), jnp.int32)
        for r in range(ROWS):
            limit = jnp.where(row == r, lengths[here + r], limit)
        visible = jnp.logical_and(offset >= 0, offset < limit[None, None])
        rows = q[pl.ds(here // 16 * 16, 16), :].astype(jnp.float32)
        rows = rows[here % 16 : here % 16 + ROWS]
        stacked = jnp.concatenate(
            [rows[:, h * 128 : (h + 1) * 128] for h in range(heads)], axis=0
        ).astype(jnp.bfloat16)
        keys = k[pl.ds(here // ROWS * span, span), :]
        values = v[pl.ds(here // ROWS * span, span), :]
        scores = lax.dot_general(
            stacked, keys, (((1,), (1,)), ((), ())), preferred_element_type=jnp.float32
        ).reshape(slot_count, per_slot, ROWS, span)
        scores = jnp.where(visible, scores, MASKED)
        top = jnp.max(scores, axis=-1, keepdims=True)
        weights = jnp.exp((scores - top) * scale).reshape(heads * ROWS, span).astype(jnp.bfloat16)
        both = jnp.concatenate([values, jnp.ones_like(values)], axis=1)
        summed = jnp.dot(weights, both, preferred_element_type=jnp.float32)
        mean = summed[:, :128] / summed[:, 128:]
        finished.append(
            jnp.concatenate([mean[h * ROWS : (h + 1) * ROWS] for h in range(heads)], axis=1)
        )
        if len(finished) == 2:
            out[pl.ds(here - ROWS, 16), :] = jnp.concatenate(finished, axis=0).astype(out.dtype)
            finished = []


class Stream:
    def __init__(self, jobs, ahead):
        self.jobs, self.ahead, self.next = jobs, ahead, 0
        for job in jobs[:ahead]:
            self.start(job)

    def start(self, job):
        for copy in job:
            copy.start()

    def take(self):
        for copy in self.jobs[self.next]:
            copy.wait()
        for job in self.jobs[self.next + self.ahead : self.next + self.ahead + 1]:
            self.start(job)
        self.next += 1


def weight_columns(step, n_chip, width, tile, weight, held, sems):
    tensor = lax.axis_index("tensor")
    chip = lax.rem(lax.div(tensor, 2) + step, n_chip)
    core = lax.rem(tensor, 2)
    jobs = []
    for number in range(2 * width // tile):
        block = chip * 2 + (1 - core if number * tile < width else core)
        start = pl.multiple_of(block * width + number * tile % width, tile)
        jobs.append(
            [
                pltpu.make_async_copy(
                    weight.at[:, pl.ds(start, tile)], held.at[number], sems.at[number]
                )
            ]
        )
    return jobs


def project_rows(x, stream, held, made, outs, sems, others=()):
    width, tile = made.shape[2], held.shape[2]
    steps = width // tile
    copies = []
    for block, out in enumerate(outs):
        for step in range(steps):
            stream.take()
            total = jnp.dot(x[...], held[block * steps + step], preferred_element_type=jnp.float32)
            made[block, :, step * tile : (step + 1) * tile] = total.astype(made.dtype)
        copy = pltpu.make_async_copy(made.at[block], out, sems.at[block])
        copy.start()
        copies.append(copy)
    for other in others:
        other.wait()
    return copies


def front_kernel(
    n_chip, n_store, slot_count, length, chunk, sends_in, lengths_in, q_in, k_in, v_in, w_in, up_in, *refs
):
    flag, attended, other, own = refs[:4]
    *singles, pair = refs[4 : 5 + n_store - CAP]
    sends, lengths, q, k, v, w, up, x, made, table_sem, qkv_sem, w_sem, up_sem, out_sem = refs[-14:]
    rows, width = q.shape[0], made.shape[2]
    per_row = slot_count * length
    jobs = []
    for part in range(rows // chunk):
        job = []
        for number, (source, held, size) in enumerate(
            ((q_in, q, chunk), (k_in, k, chunk * per_row), (v_in, v, chunk * per_row))
        ):
            span = pl.ds(part * size, size)
            job.append(
                pltpu.make_async_copy(source.at[span], held.at[span], qkv_sem.at[part, number])
            )
        jobs.append(job)
    jobs[0].append(pltpu.make_async_copy(lengths_in, lengths, table_sem.at[0]))
    jobs[0].append(pltpu.make_async_copy(sends_in, sends, table_sem.at[1]))
    stream = Stream(
        jobs + weight_columns(1, n_chip, width, w.shape[2], w_in, w, w_sem), AHEAD
    )
    span = ROWS * per_row
    shape = (slot_count, 1, ROWS, span)
    offset = (
        lax.broadcasted_iota(jnp.int32, shape, 3)
        - lax.broadcasted_iota(jnp.int32, shape, 2) * per_row
        - lax.broadcasted_iota(jnp.int32, shape, 0) * length
    )
    row = lax.broadcasted_iota(jnp.int32, (ROWS, span), 0)
    for part in range(rows // chunk):
        stream.take()
        attend_rows(part * chunk, chunk, lengths, q, k, v, x, slot_count, length, offset, row)
    flag[0] = lengths[0]
    slabs = []
    for slot in range(n_store):
        slab = pltpu.make_async_copy(up_in.at[sends[slot]], up.at[slot], up_sem.at[slot])
        slab.start()
        slabs.append(slab)
    copies = [pltpu.make_async_copy(x, attended, out_sem.at[2])]
    copies[0].start()
    copies += project_rows(x, stream, w, made, (other, own), out_sem, slabs)
    targets = list(singles) + [pair.at[rank] for rank in range(CAP)]
    for slot, target in enumerate(targets):
        copies.append(pltpu.make_async_copy(up.at[slot], target, up_sem.at[slot]))
        copies[-1].start()
    for copy in copies:
        copy.wait()


def front(n_chip, n_store, sends, lengths, queries, keys, values, weight, up):
    width = up.shape[2]
    slab = jax.ShapeDtypeStruct(up.shape[1:], up.dtype)
    pair = jax.ShapeDtypeStruct((CAP,) + up.shape[1:], up.dtype)
    rows, slot_count, length, head = keys.shape
    depth = queries.shape[1]
    tile = min(512, width)
    tiles = 2 * width // tile
    chunk = min(CHUNK, rows)
    half = jax.ShapeDtypeStruct((rows, width), jnp.bfloat16)
    return pl.pallas_call(
        functools.partial(front_kernel, n_chip, n_store, slot_count, length, chunk),
        out_shape=[
            jax.ShapeDtypeStruct((1,), jnp.int32),
            jax.ShapeDtypeStruct((rows, depth), jnp.bfloat16),
            half,
            half,
        ]
        + [slab] * (n_store - CAP)
        + [pair],
        in_specs=[ANY] * 2 + [HBM] * 5,
        out_specs=[SMEM] + [ANY] * (4 + n_store - CAP),
        scratch_shapes=[
            pltpu.SMEM(sends.shape, sends.dtype),
            pltpu.SMEM(lengths.shape, lengths.dtype),
            pltpu.VMEM((rows, depth), queries.dtype),
            pltpu.VMEM((rows * slot_count * length, head), keys.dtype),
            pltpu.VMEM((rows * slot_count * length, head), values.dtype),
            pltpu.VMEM((tiles, depth, tile), weight.dtype),
            pltpu.VMEM((n_store,) + up.shape[1:], up.dtype),
            pltpu.VMEM((rows, depth), jnp.bfloat16),
            pltpu.VMEM((2, rows, width), jnp.bfloat16),
            pltpu.SemaphoreType.DMA((2,)),
            pltpu.SemaphoreType.DMA((rows // chunk, 3)),
            pltpu.SemaphoreType.DMA((tiles,)),
            pltpu.SemaphoreType.DMA((n_store,)),
            pltpu.SemaphoreType.DMA((3,)),
        ],
        compiler_params=params(58),
        cost_estimate=SMALL,
        name="front",
    )(
        sends,
        lengths,
        queries,
        keys.reshape(-1, head),
        values.reshape(-1, head),
        weight,
        up,
    )


def project_kernel(step, n_chip, x, w_in, *refs):
    other, own, w, made, w_sem, out_sem = refs[-6:]
    stream = Stream(
        weight_columns(step, n_chip, made.shape[2], w.shape[2], w_in, w, w_sem), AHEAD
    )
    for copy in project_rows(x, stream, w, made, (other, own), out_sem):
        copy.wait()


def project(step, n_chip, attended, weight, width, *earlier):
    rows, depth = attended.shape
    tile = min(512, width)
    tiles = 2 * width // tile
    half = jax.ShapeDtypeStruct((rows, width), jnp.bfloat16)
    return pl.pallas_call(
        functools.partial(project_kernel, step, n_chip),
        out_shape=[half, half],
        in_specs=[VMEM, HBM] + [ANY] * len(earlier),
        out_specs=[ANY] * 2,
        scratch_shapes=[
            pltpu.VMEM((tiles, depth, tile), weight.dtype),
            pltpu.VMEM((2, rows, width), jnp.bfloat16),
            pltpu.SemaphoreType.DMA((tiles,)),
            pltpu.SemaphoreType.DMA((2,)),
        ],
        compiler_params=params(26),
        cost_estimate=SMALL,
        name="project",
    )(attended, weight, *earlier)


def place_row(info, entries):
    place = jnp.zeros(entries.shape, jnp.int32)
    for entry in range(info.shape[0] - CAP):
        place = jnp.where(entries == entry, info[CAP + entry], place)
    return place


def shrink_kernel(count, info, entries_ref, x_ref, near_ref, *refs):
    slab_refs, (o_ref, near, sem) = refs[:count], refs[-3:]
    fetches = []
    for rank in range(CAP):
        fetch = pltpu.make_async_copy(near_ref.at[info[rank]], near.at[rank], sem.at[rank])
        fetch.start()
        fetches.append(fetch)
    place = place_row(info, entries_ref[...])
    for fetch in fetches:
        fetch.wait()
    slabs = jnp.concatenate(
        [near[rank] for rank in range(CAP)]
        + [ref[...].reshape(-1, ref.shape[-1]) for ref in slab_refs],
        axis=0,
    )
    products = lax.dot_general(
        slabs, x_ref[...], (((1,), (1,)), ((), ())), preferred_element_type=jnp.float32
    )
    size = o_ref.shape[0]
    total = jnp.zeros(o_ref.shape, jnp.float32)
    for slot in range(slabs.shape[0] // size):
        total = total + jnp.where(place == slot, products[slot * size : (slot + 1) * size], 0.0)
    o_ref[...] = total


def shrink_part(info, entries, attended, near, slabs, *earlier):
    rows = attended.shape[0]
    _, size, width = near.shape
    return pl.pallas_call(
        functools.partial(shrink_kernel, len(slabs)),
        out_shape=jax.ShapeDtypeStruct((size, rows), jnp.float32),
        in_specs=[SMEM, VMEM, VMEM, HBM] + [VMEM] * len(slabs) + [ANY] * len(earlier),
        out_specs=VMEM,
        scratch_shapes=[
            pltpu.VMEM((CAP, size, width), near.dtype),
            pltpu.SemaphoreType.DMA((CAP,)),
        ],
        compiler_params=params(14),
        cost_estimate=SMALL,
        name="shrink",
    )(info, entries, attended, near, *slabs, *earlier)


def spread_kernel(slot_total, info, entries_ref, parts_ref, *refs):
    o_ref = refs[-1]
    place = place_row(info, entries_ref[...])
    low = jnp.sum(parts_ref[...].astype(jnp.float32), axis=0).astype(jnp.bfloat16).astype(jnp.float32)
    wide = jnp.concatenate(
        [jnp.where(place == slot, low, 0.0) for slot in range(slot_total)], axis=0
    )
    o_ref[...] = wide.T.astype(jnp.bfloat16)


def spread(info, entries, parts, slot_total, *earlier):
    _, size, rows = parts.shape
    return pl.pallas_call(
        functools.partial(spread_kernel, slot_total),
        out_shape=jax.ShapeDtypeStruct((rows, slot_total * size), jnp.bfloat16),
        in_specs=[SMEM, VMEM, VMEM] + [ANY] * len(earlier),
        out_specs=VMEM,
        compiler_params=params(12),
        cost_estimate=pl.CostEstimate(flops=1, bytes_accessed=8000000, transcendentals=0),
        name="spread",
    )(info, entries, parts, *earlier)


def expand_kernel(count, part_count, info, wide_ref, near_ref, *refs):
    slab_refs, parts = refs[:count], refs[count : count + sum(part_count)]
    o_ref, near, sem = refs[-3:]
    fetches = []
    for rank in range(CAP):
        fetch = pltpu.make_async_copy(near_ref.at[info[rank]], near.at[rank], sem.at[rank])
        fetch.start()
        fetches.append(fetch)
    for fetch in fetches:
        fetch.wait()
    slabs = jnp.concatenate(
        [near[rank] for rank in range(CAP)]
        + [ref[...].reshape(-1, ref.shape[-1]) for ref in slab_refs],
        axis=0,
    )
    total = jnp.dot(
        wide_ref[:, : slabs.shape[0]], slabs, preferred_element_type=jnp.float32
    )
    rest = iter(parts)
    for pieces in part_count:
        part = jnp.concatenate([next(rest)[...] for _ in range(pieces)], axis=0)
        total = total + part.astype(jnp.float32)
    o_ref[...] = total.astype(o_ref.dtype)


def expand(info, wide, near, slabs, parts, *earlier):
    rows, width = parts[0][0].shape
    counts = [len(pieces) for pieces in parts]
    flat = [piece for pieces in parts for piece in pieces]
    return pl.pallas_call(
        functools.partial(expand_kernel, len(slabs), counts),
        out_shape=jax.ShapeDtypeStruct((rows, width), jnp.float32),
        in_specs=[SMEM, VMEM, HBM] + [VMEM] * (len(slabs) + len(flat)) + [ANY] * len(earlier),
        out_specs=VMEM,
        scratch_shapes=[
            pltpu.VMEM((CAP,) + near.shape[1:], near.dtype),
            pltpu.SemaphoreType.DMA((CAP,)),
        ],
        compiler_params=params(14),
        cost_estimate=SMALL,
        name="expand",
    )(info, wide, near, *slabs, *flat, *earlier)


def finish_kernel(wide_ref, total_ref, *refs):
    slab_ref, o_ref, made, sems = refs
    first = wide_ref.shape[1] - slab_ref.shape[0]
    width = made.shape[1]
    tile = min(512, width)
    copies = []
    for number in range(width // tile):
        span = pl.ds(number * tile, tile)
        delta = jnp.dot(
            wide_ref[:, first:], slab_ref[:, span], preferred_element_type=jnp.float32
        )
        made[:, span] = (total_ref[:, span] + delta).astype(made.dtype)
        copies.append(pltpu.make_async_copy(made.at[:, span], o_ref.at[:, span], sems.at[number]))
        copies[-1].start()
    for copy in copies:
        copy.wait()


def finish(wide, total, slab):
    width = total.shape[1]
    return pl.pallas_call(
        finish_kernel,
        out_shape=jax.ShapeDtypeStruct(total.shape, jnp.bfloat16),
        in_specs=[VMEM] * 3,
        out_specs=ANY,
        scratch_shapes=[
            pltpu.VMEM(total.shape, jnp.bfloat16),
            pltpu.SemaphoreType.DMA((width // min(512, width),)),
        ],
        compiler_params=params(14),
        cost_estimate=SMALL,
        name="finish",
    )(wide, total, slab)


def shards(
    mesh,
    queries,
    cached_key_slabs,
    cached_value_slabs,
    request_cache_lengths,
    output_projection_weight,
    adapter_shrink_weight,
    adapter_expand_weight,
    adapter_storage_slot,
    wanted,
    request_wanted_entry,
):
    n_store, n_tensor = mesh.shape["store"], mesh.shape["tensor"]
    n_chip = n_tensor // 2
    local_width = adapter_shrink_weight.shape[2]
    far_steps = range(1, n_chip)

    def along_store(x, step):
        return lax.ppermute(x, "store", [(s, s ^ step) for s in range(n_store)])

    def swap_group(x):
        return lax.ppermute(x, "group", [(0, 1), (1, 0)])

    def swap_core(x):
        return lax.ppermute(x, "tensor", [(t, t ^ 1) for t in range(n_tensor)])

    def along_chip(x, step):
        return lax.ppermute(x, "tensor", [(t, (t + 2 * step) % n_tensor) for t in range(n_tensor)])

    weight = output_projection_weight
    *picked, info, sends = pick(adapter_storage_slot, wanted, adapter_shrink_weight)
    steps = range(CAP, n_store)
    next_down = [along_store(x, 1) for x in picked[len(steps) : n_store]]
    own_down = [along_store(x, step) for step, x in zip(steps, picked)]
    flag, attended, other, own, *send_up, send_pair = front(
        n_chip,
        n_store,
        sends,
        request_cache_lengths,
        queries,
        cached_key_slabs,
        cached_value_slabs,
        weight,
        adapter_expand_weight,
    )

    def meet(mine, given):
        return (mine.astype(jnp.float32) + given.astype(jnp.float32)).astype(jnp.bfloat16)

    def join(other, own):
        return lax.cond(
            flag[0] > 0,
            lambda: meet(own, swap_core(other)),
            lambda: meet(swap_core(other), own),
        )

    arrived = []
    for step in far_steps:
        if step > 1:
            other, own = project(step, n_chip, attended, weight, local_width, met)
        met = join(other, own)
        arrived.append([along_chip(met, step)])
    own_up = [along_store(tie(x, met), step) for step, x in zip(steps, send_up)]
    next_up = along_store(tie(send_pair, met), 1)
    own_down = tie(stack(own_down, met), *next_down)
    swapped_down = swap_group(own_down)
    other, own = project(0, n_chip, attended, weight, local_width, met)

    def middle(first):
        given = swap_core(other)
        swapped = [swap_group(x) for x in own_up[:-1]]
        part = shrink_part(
            info,
            request_wanted_entry,
            attended,
            adapter_shrink_weight,
            [*next_down, own_down, swapped_down],
        )
        base = meet(own, given) if first else meet(given, own)
        return base, swapped, lax.all_gather(part.astype(jnp.bfloat16), "tensor")

    base, swapped_up, gathered = lax.cond(
        flag[0] > 0, lambda: middle(True), lambda: middle(False)
    )
    wide = spread(info, request_wanted_entry, gathered, n_store * CAP)
    last = tie(own_up[-1], wide)
    swapped = swap_group(last)
    total = expand(
        info,
        wide,
        adapter_expand_weight,
        [next_up] + own_up[:-1] + [last] + swapped_up,
        [[base]] + arrived,
    )
    return finish(wide, total, swapped)


def solution(mesh):
    placed = (
        P(("group", "store"), "tensor"),
        P(("group", "store"), "tensor", None, None),
        P(("group", "store"), "tensor", None, None),
        P(("group", "store")),
        P("tensor", None),
        P("store", None, "tensor"),
        P("store", None, "tensor"),
        P(),
        P(),
        P(("group", "store"), None),
    )
    return jax.shard_map(
        functools.partial(shards, mesh),
        mesh=mesh,
        in_specs=placed,
        out_specs=P(("group", "store"), "tensor"),
        check_vma=False,
    )
```

```python
import functools
import math

import jax
import jax.numpy as jnp
from jax import lax
from jax.experimental import pallas as pl
from jax.experimental.pallas import tpu as pltpu
from jax.sharding import PartitionSpec as P

CAP = 2
ROWS = 8
MASKED = -1e30
AHEAD = 4
CHUNK = 128
MIB = 1 << 20
ANY = pl.BlockSpec(memory_space=pl.ANY)
HBM = pl.BlockSpec(memory_space=pltpu.HBM)
SMEM = pl.BlockSpec(memory_space=pltpu.SMEM)
VMEM = pl.BlockSpec(memory_space=pltpu.VMEM)


SMALL = pl.CostEstimate(flops=1, bytes_accessed=1, transcendentals=0)


def params(mib=56):
    return pltpu.CompilerParams(vmem_limit_bytes=mib * MIB)


def held_index(slots, wanted, row, holder, rank, per_store):
    index = jnp.int32(0)
    count = jnp.int32(0)
    for entry in range(wanted.shape[1]):
        local = slots[wanted[row, entry]] - holder * per_store
        held = jnp.logical_and(local >= 0, local < per_store)
        index = jnp.where(jnp.logical_and(held, count == rank), local, index)
        count = count + held.astype(jnp.int32)
    return index


def pick_kernel(n_store, slots_in, wanted_in, down, *refs):
    outs, (info, sends, slots, wanted, held, table_sem, in_sem, out_sem) = refs[:-8], refs[-8:]
    tables = [
        pltpu.make_async_copy(slots_in, slots, table_sem.at[0]),
        pltpu.make_async_copy(wanted_in, wanted, table_sem.at[1]),
    ]
    for table in tables:
        table.start()
    for table in tables:
        table.wait()
    store, group = lax.axis_index("store"), lax.axis_index("group")
    per_store = down.shape[0]
    indices = [
        held_index(slots, wanted, store ^ step, store, group, per_store)
        for step in range(CAP, n_store)
    ]
    indices += [
        held_index(slots, wanted, store ^ 1, store, rank, per_store) for rank in range(CAP)
    ]
    fetches = []
    for slot, index in enumerate(indices):
        fetch = pltpu.make_async_copy(down.at[index], held.at[slot], in_sem.at[slot])
        fetch.start()
        fetches.append(fetch)
        sends[slot] = index
    for rank in range(CAP):
        info[rank] = held_index(slots, wanted, store, store, rank, per_store)
    copies = []
    for slot, target in enumerate(outs):
        fetches[slot].wait()
        copies.append(pltpu.make_async_copy(held.at[slot], target, out_sem.at[slot]))
        copies[-1].start()
    used = wanted.shape[1]
    holders = [lax.div(slots[wanted[store, entry]], per_store) for entry in range(used)]
    for entry in range(used):
        rank = jnp.int32(0)
        for earlier in range(entry):
            rank = rank + (holders[earlier] == holders[entry]).astype(jnp.int32)
        step = store ^ holders[entry]
        far = CAP + step + jnp.where(rank == group, 0, n_store - CAP)
        info[CAP + entry] = jnp.where(step <= 1, step * CAP + rank, far)
    for copy in copies:
        copy.wait()


def pick(slots, wanted, down):
    n_store = wanted.shape[0]
    slab = jax.ShapeDtypeStruct(down.shape[1:], down.dtype)
    return pl.pallas_call(
        functools.partial(pick_kernel, n_store),
        out_shape=[slab] * n_store
        + [
            jax.ShapeDtypeStruct((CAP + wanted.shape[1],), jnp.int32),
            jax.ShapeDtypeStruct((n_store,), jnp.int32),
        ],
        in_specs=[ANY, ANY, HBM],
        out_specs=[ANY] * n_store + [SMEM, SMEM],
        scratch_shapes=[
            pltpu.SMEM(slots.shape, slots.dtype),
            pltpu.SMEM(wanted.shape, wanted.dtype),
            pltpu.VMEM((n_store,) + down.shape[1:], down.dtype),
            pltpu.SemaphoreType.DMA((2,)),
            pltpu.SemaphoreType.DMA((n_store,)),
            pltpu.SemaphoreType.DMA((n_store,)),
        ],
        compiler_params=params(62),
        cost_estimate=SMALL,
        name="pick",
    )(slots, wanted, down)


def stack_kernel(count, *refs):
    o_ref = refs[-1]
    slabs = refs[-1 - count : -1]
    for number in range(count):
        o_ref[number] = slabs[number][...]


def stack(slabs, *earlier):
    return pl.pallas_call(
        functools.partial(stack_kernel, len(slabs)),
        out_shape=jax.ShapeDtypeStruct((len(slabs),) + slabs[0].shape, slabs[0].dtype),
        in_specs=[ANY] * len(earlier) + [VMEM] * len(slabs),
        out_specs=VMEM,
        compiler_params=params(8),
        cost_estimate=SMALL,
        name="stack",
    )(*earlier, *slabs)


def tie_kernel(*refs):
    pass


def tie(value, *earlier):
    return pl.pallas_call(
        tie_kernel,
        out_shape=jax.ShapeDtypeStruct(value.shape, value.dtype),
        in_specs=[ANY] * (1 + len(earlier)),
        out_specs=ANY,
        input_output_aliases={0: 0},
        compiler_params=params(2),
        cost_estimate=SMALL,
        name="tie",
    )(value, *earlier)


def attend_rows(first, count, lengths, q, k, v, out, slot_count, length, offset, row):
    heads = q.shape[1] // 128
    per_slot = heads // slot_count
    span = ROWS * slot_count * length
    scale = 1.0 / math.sqrt(128)
    finished = []
    for here in range(first, first + count, ROWS):
        limit = jnp.zeros((ROWS, span), jnp.int32)
        for r in range(ROWS):
            limit = jnp.where(row == r, lengths[here + r], limit)
        visible = jnp.logical_and(offset >= 0, offset < limit[None, None])
        rows = q[pl.ds(here // 16 * 16, 16), :].astype(jnp.float32)
        rows = rows[here % 16 : here % 16 + ROWS]
        stacked = jnp.concatenate(
            [rows[:, h * 128 : (h + 1) * 128] for h in range(heads)], axis=0
        ).astype(jnp.bfloat16)
        keys = k[pl.ds(here // ROWS * span, span), :]
        values = v[pl.ds(here // ROWS * span, span), :]
        scores = lax.dot_general(
            stacked, keys, (((1,), (1,)), ((), ())), preferred_element_type=jnp.float32
        ).reshape(slot_count, per_slot, ROWS, span)
        scores = jnp.where(visible, scores, MASKED)
        top = jnp.max(scores, axis=-1, keepdims=True)
        weights = jnp.exp((scores - top) * scale).reshape(heads * ROWS, span).astype(jnp.bfloat16)
        both = jnp.concatenate([values, jnp.ones_like(values)], axis=1)
        summed = jnp.dot(weights, both, preferred_element_type=jnp.float32)
        mean = summed[:, :128] / summed[:, 128:]
        finished.append(
            jnp.concatenate([mean[h * ROWS : (h + 1) * ROWS] for h in range(heads)], axis=1)
        )
        if len(finished) == 2:
            out[pl.ds(here - ROWS, 16), :] = jnp.concatenate(finished, axis=0).astype(out.dtype)
            finished = []


class Stream:
    def __init__(self, jobs, ahead):
        self.jobs, self.ahead, self.next = jobs, ahead, 0
        for job in jobs[:ahead]:
            self.start(job)

    def start(self, job):
        for copy in job:
            copy.start()

    def take(self):
        for copy in self.jobs[self.next]:
            copy.wait()
        for job in self.jobs[self.next + self.ahead : self.next + self.ahead + 1]:
            self.start(job)
        self.next += 1


def weight_columns(step, n_chip, width, tile, weight, held, sems):
    tensor = lax.axis_index("tensor")
    chip = lax.rem(lax.div(tensor, 2) + step, n_chip)
    core = lax.rem(tensor, 2)
    jobs = []
    for number in range(2 * width // tile):
        block = chip * 2 + (1 - core if number * tile < width else core)
        start = pl.multiple_of(block * width + number * tile % width, tile)
        jobs.append(
            [
                pltpu.make_async_copy(
                    weight.at[:, pl.ds(start, tile)], held.at[number], sems.at[number]
                )
            ]
        )
    return jobs


def project_rows(x, stream, held, made, outs, sems, others=()):
    width, tile = made.shape[2], held.shape[2]
    steps = width // tile
    copies = []
    for block, out in enumerate(outs):
        for step in range(steps):
            stream.take()
            total = jnp.dot(x[...], held[block * steps + step], preferred_element_type=jnp.float32)
            made[block, :, step * tile : (step + 1) * tile] = total.astype(made.dtype)
        copy = pltpu.make_async_copy(made.at[block], out, sems.at[block])
        copy.start()
        copies.append(copy)
    for other in others:
        other.wait()
    return copies


def front_kernel(
    n_chip, n_store, slot_count, length, chunk, sends_in, lengths_in, q_in, k_in, v_in, w_in, up_in, *refs
):
    flag, attended, other, own = refs[:4]
    *singles, pair = refs[4 : 5 + n_store - CAP]
    sends, lengths, q, k, v, w, up, x, made, table_sem, qkv_sem, w_sem, up_sem, out_sem = refs[-14:]
    rows, width = q.shape[0], made.shape[2]
    per_row = slot_count * length
    jobs = []
    for part in range(rows // chunk):
        job = []
        for number, (source, held, size) in enumerate(
            ((q_in, q, chunk), (k_in, k, chunk * per_row), (v_in, v, chunk * per_row))
        ):
            span = pl.ds(part * size, size)
            job.append(
                pltpu.make_async_copy(source.at[span], held.at[span], qkv_sem.at[part, number])
            )
        jobs.append(job)
    jobs[0].append(pltpu.make_async_copy(lengths_in, lengths, table_sem.at[0]))
    jobs[0].append(pltpu.make_async_copy(sends_in, sends, table_sem.at[1]))
    stream = Stream(
        jobs + weight_columns(1, n_chip, width, w.shape[2], w_in, w, w_sem), AHEAD
    )
    span = ROWS * per_row
    shape = (slot_count, 1, ROWS, span)
    offset = (
        lax.broadcasted_iota(jnp.int32, shape, 3)
        - lax.broadcasted_iota(jnp.int32, shape, 2) * per_row
        - lax.broadcasted_iota(jnp.int32, shape, 0) * length
    )
    row = lax.broadcasted_iota(jnp.int32, (ROWS, span), 0)
    for part in range(rows // chunk):
        stream.take()
        attend_rows(part * chunk, chunk, lengths, q, k, v, x, slot_count, length, offset, row)
    flag[0] = lengths[0]
    slabs = []
    for slot in range(n_store):
        slab = pltpu.make_async_copy(up_in.at[sends[slot]], up.at[slot], up_sem.at[slot])
        slab.start()
        slabs.append(slab)
    copies = [pltpu.make_async_copy(x, attended, out_sem.at[2])]
    copies[0].start()
    copies += project_rows(x, stream, w, made, (other, own), out_sem, slabs)
    targets = list(singles) + [pair.at[rank] for rank in range(CAP)]
    for slot, target in enumerate(targets):
        copies.append(pltpu.make_async_copy(up.at[slot], target, up_sem.at[slot]))
        copies[-1].start()
    for copy in copies:
        copy.wait()


def front(n_chip, n_store, sends, lengths, queries, keys, values, weight, up):
    width = up.shape[2]
    slab = jax.ShapeDtypeStruct(up.shape[1:], up.dtype)
    pair = jax.ShapeDtypeStruct((CAP,) + up.shape[1:], up.dtype)
    rows, slot_count, length, head = keys.shape
    depth = queries.shape[1]
    tile = min(512, width)
    tiles = 2 * width // tile
    chunk = min(CHUNK, rows)
    half = jax.ShapeDtypeStruct((rows, width), jnp.bfloat16)
    return pl.pallas_call(
        functools.partial(front_kernel, n_chip, n_store, slot_count, length, chunk),
        out_shape=[
            jax.ShapeDtypeStruct((1,), jnp.int32),
            jax.ShapeDtypeStruct((rows, depth), jnp.bfloat16),
            half,
            half,
        ]
        + [slab] * (n_store - CAP)
        + [pair],
        in_specs=[ANY] * 2 + [HBM] * 5,
        out_specs=[SMEM] + [ANY] * (4 + n_store - CAP),
        scratch_shapes=[
            pltpu.SMEM(sends.shape, sends.dtype),
            pltpu.SMEM(lengths.shape, lengths.dtype),
            pltpu.VMEM((rows, depth), queries.dtype),
            pltpu.VMEM((rows * slot_count * length, head), keys.dtype),
            pltpu.VMEM((rows * slot_count * length, head), values.dtype),
            pltpu.VMEM((tiles, depth, tile), weight.dtype),
            pltpu.VMEM((n_store,) + up.shape[1:], up.dtype),
            pltpu.VMEM((rows, depth), jnp.bfloat16),
            pltpu.VMEM((2, rows, width), jnp.bfloat16),
            pltpu.SemaphoreType.DMA((2,)),
            pltpu.SemaphoreType.DMA((rows // chunk, 3)),
            pltpu.SemaphoreType.DMA((tiles,)),
            pltpu.SemaphoreType.DMA((n_store,)),
            pltpu.SemaphoreType.DMA((3,)),
        ],
        compiler_params=params(58),
        cost_estimate=SMALL,
        name="front",
    )(
        sends,
        lengths,
        queries,
        keys.reshape(-1, head),
        values.reshape(-1, head),
        weight,
        up,
    )


def project_kernel(step, n_chip, x, w_in, *refs):
    other, own, w, made, w_sem, out_sem = refs[-6:]
    stream = Stream(
        weight_columns(step, n_chip, made.shape[2], w.shape[2], w_in, w, w_sem), AHEAD
    )
    for copy in project_rows(x, stream, w, made, (other, own), out_sem):
        copy.wait()


def project(step, n_chip, attended, weight, width, *earlier):
    rows, depth = attended.shape
    tile = min(512, width)
    tiles = 2 * width // tile
    half = jax.ShapeDtypeStruct((rows, width), jnp.bfloat16)
    return pl.pallas_call(
        functools.partial(project_kernel, step, n_chip),
        out_shape=[half, half],
        in_specs=[VMEM, HBM] + [ANY] * len(earlier),
        out_specs=[ANY] * 2,
        scratch_shapes=[
            pltpu.VMEM((tiles, depth, tile), weight.dtype),
            pltpu.VMEM((2, rows, width), jnp.bfloat16),
            pltpu.SemaphoreType.DMA((tiles,)),
            pltpu.SemaphoreType.DMA((2,)),
        ],
        compiler_params=params(26),
        cost_estimate=SMALL,
        name="project",
    )(attended, weight, *earlier)


def place_row(info, entries):
    place = jnp.zeros(entries.shape, jnp.int32)
    for entry in range(info.shape[0] - CAP):
        place = jnp.where(entries == entry, info[CAP + entry], place)
    return place


def shrink_kernel(count, info, entries_ref, x_ref, near_ref, *refs):
    slab_refs, (o_ref, near, sem) = refs[:count], refs[-3:]
    fetches = []
    for rank in range(CAP):
        fetch = pltpu.make_async_copy(near_ref.at[info[rank]], near.at[rank], sem.at[rank])
        fetch.start()
        fetches.append(fetch)
    place = place_row(info, entries_ref[...])
    for fetch in fetches:
        fetch.wait()
    slabs = jnp.concatenate(
        [near[rank] for rank in range(CAP)]
        + [ref[...].reshape(-1, ref.shape[-1]) for ref in slab_refs],
        axis=0,
    )
    products = lax.dot_general(
        slabs, x_ref[...], (((1,), (1,)), ((), ())), preferred_element_type=jnp.float32
    )
    size = o_ref.shape[0]
    total = jnp.zeros(o_ref.shape, jnp.float32)
    for slot in range(slabs.shape[0] // size):
        total = total + jnp.where(place == slot, products[slot * size : (slot + 1) * size], 0.0)
    o_ref[...] = total


def shrink_part(info, entries, attended, near, slabs, *earlier):
    rows = attended.shape[0]
    _, size, width = near.shape
    return pl.pallas_call(
        functools.partial(shrink_kernel, len(slabs)),
        out_shape=jax.ShapeDtypeStruct((size, rows), jnp.float32),
        in_specs=[SMEM, VMEM, VMEM, HBM] + [VMEM] * len(slabs) + [ANY] * len(earlier),
        out_specs=VMEM,
        scratch_shapes=[
            pltpu.VMEM((CAP, size, width), near.dtype),
            pltpu.SemaphoreType.DMA((CAP,)),
        ],
        compiler_params=params(14),
        cost_estimate=SMALL,
        name="shrink",
    )(info, entries, attended, near, *slabs, *earlier)


def spread_kernel(slot_total, info, entries_ref, parts_ref, *refs):
    o_ref = refs[-1]
    place = place_row(info, entries_ref[...])
    low = jnp.sum(parts_ref[...].astype(jnp.float32), axis=0).astype(jnp.bfloat16).astype(jnp.float32)
    wide = jnp.concatenate(
        [jnp.where(place == slot, low, 0.0) for slot in range(slot_total)], axis=0
    )
    o_ref[...] = wide.T.astype(jnp.bfloat16)


def spread(info, entries, parts, slot_total, *earlier):
    _, size, rows = parts.shape
    return pl.pallas_call(
        functools.partial(spread_kernel, slot_total),
        out_shape=jax.ShapeDtypeStruct((rows, slot_total * size), jnp.bfloat16),
        in_specs=[SMEM, VMEM, VMEM] + [ANY] * len(earlier),
        out_specs=VMEM,
        compiler_params=params(12),
        cost_estimate=pl.CostEstimate(flops=1, bytes_accessed=8000000, transcendentals=0),
        name="spread",
    )(info, entries, parts, *earlier)


def expand_kernel(count, part_count, info, wide_ref, near_ref, *refs):
    slab_refs, parts = refs[:count], refs[count : count + sum(part_count)]
    o_ref, near, sem = refs[-3:]
    fetches = []
    for rank in range(CAP):
        fetch = pltpu.make_async_copy(near_ref.at[info[rank]], near.at[rank], sem.at[rank])
        fetch.start()
        fetches.append(fetch)
    for fetch in fetches:
        fetch.wait()
    slabs = jnp.concatenate(
        [near[rank] for rank in range(CAP)]
        + [ref[...].reshape(-1, ref.shape[-1]) for ref in slab_refs],
        axis=0,
    )
    total = jnp.dot(
        wide_ref[:, : slabs.shape[0]], slabs, preferred_element_type=jnp.float32
    )
    rest = iter(parts)
    for pieces in part_count:
        part = jnp.concatenate([next(rest)[...] for _ in range(pieces)], axis=0)
        total = total + part.astype(jnp.float32)
    o_ref[...] = total.astype(o_ref.dtype)


def expand(info, wide, near, slabs, parts, *earlier):
    rows, width = parts[0][0].shape
    counts = [len(pieces) for pieces in parts]
    flat = [piece for pieces in parts for piece in pieces]
    return pl.pallas_call(
        functools.partial(expand_kernel, len(slabs), counts),
        out_shape=jax.ShapeDtypeStruct((rows, width), jnp.float32),
        in_specs=[SMEM, VMEM, HBM] + [VMEM] * (len(slabs) + len(flat)) + [ANY] * len(earlier),
        out_specs=VMEM,
        scratch_shapes=[
            pltpu.VMEM((CAP,) + near.shape[1:], near.dtype),
            pltpu.SemaphoreType.DMA((CAP,)),
        ],
        compiler_params=params(14),
        cost_estimate=SMALL,
        name="expand",
    )(info, wide, near, *slabs, *flat, *earlier)


def finish_kernel(wide_ref, total_ref, *refs):
    slab_ref, o_ref, made, sems = refs
    first = wide_ref.shape[1] - slab_ref.shape[0]
    width = made.shape[1]
    tile = min(512, width)
    copies = []
    for number in range(width // tile):
        span = pl.ds(number * tile, tile)
        delta = jnp.dot(
            wide_ref[:, first:], slab_ref[:, span], preferred_element_type=jnp.float32
        )
        made[:, span] = (total_ref[:, span] + delta).astype(made.dtype)
        copies.append(pltpu.make_async_copy(made.at[:, span], o_ref.at[:, span], sems.at[number]))
        copies[-1].start()
    for copy in copies:
        copy.wait()


def finish(wide, total, slab):
    width = total.shape[1]
    return pl.pallas_call(
        finish_kernel,
        out_shape=jax.ShapeDtypeStruct(total.shape, jnp.bfloat16),
        in_specs=[VMEM] * 3,
        out_specs=ANY,
        scratch_shapes=[
            pltpu.VMEM(total.shape, jnp.bfloat16),
            pltpu.SemaphoreType.DMA((width // min(512, width),)),
        ],
        compiler_params=params(14),
        cost_estimate=SMALL,
        name="finish",
    )(wide, total, slab)


def shards(
    mesh,
    queries,
    cached_key_slabs,
    cached_value_slabs,
    request_cache_lengths,
    output_projection_weight,
    adapter_shrink_weight,
    adapter_expand_weight,
    adapter_storage_slot,
    wanted,
    request_wanted_entry,
):
    n_store, n_tensor = mesh.shape["store"], mesh.shape["tensor"]
    n_chip = n_tensor // 2
    local_width = adapter_shrink_weight.shape[2]
    far_steps = range(1, n_chip)

    def along_store(x, step):
        return lax.ppermute(x, "store", [(s, s ^ step) for s in range(n_store)])

    def swap_group(x):
        return lax.ppermute(x, "group", [(0, 1), (1, 0)])

    def swap_core(x):
        return lax.ppermute(x, "tensor", [(t, t ^ 1) for t in range(n_tensor)])

    def along_chip(x, step):
        return lax.ppermute(x, "tensor", [(t, (t + 2 * step) % n_tensor) for t in range(n_tensor)])

    weight = output_projection_weight
    *picked, info, sends = pick(adapter_storage_slot, wanted, adapter_shrink_weight)
    steps = range(CAP, n_store)
    next_down = [along_store(x, 1) for x in picked[len(steps) : n_store]]
    own_down = [along_store(x, step) for step, x in zip(steps, picked)]
    flag, attended, other, own, *send_up, send_pair = front(
        n_chip,
        n_store,
        sends,
        request_cache_lengths,
        queries,
        cached_key_slabs,
        cached_value_slabs,
        weight,
        adapter_expand_weight,
    )

    def meet(mine, given):
        return (mine.astype(jnp.float32) + given.astype(jnp.float32)).astype(jnp.bfloat16)

    def join(other, own):
        return lax.cond(
            flag[0] > 0,
            lambda: meet(own, swap_core(other)),
            lambda: meet(swap_core(other), own),
        )

    arrived = []
    for step in far_steps:
        if step > 1:
            other, own = project(step, n_chip, attended, weight, local_width, met)
        met = join(other, own)
        arrived.append([along_chip(met, step)])
    own_up = [along_store(tie(x, met), step) for step, x in zip(steps, send_up)]
    next_up = along_store(tie(send_pair, met), 1)
    own_down = tie(stack(own_down, met), *next_down)
    swapped_down = swap_group(own_down)
    other, own = project(0, n_chip, attended, weight, local_width, met)

    def middle(first):
        given = swap_core(other)
        swapped = [swap_group(x) for x in own_up[:-1]]
        part = shrink_part(
            info,
            request_wanted_entry,
            attended,
            adapter_shrink_weight,
            [*next_down, own_down, swapped_down],
        )
        base = meet(own, given) if first else meet(given, own)
        return base, swapped, lax.all_gather(part.astype(jnp.bfloat16), "tensor")

    base, swapped_up, gathered = lax.cond(
        flag[0] > 0, lambda: middle(True), lambda: middle(False)
    )
    wide = spread(info, request_wanted_entry, gathered, n_store * CAP, own_up[-1])
    last = tie(own_up[-1], wide)
    swapped = swap_group(last)
    total = expand(
        info,
        wide,
        adapter_expand_weight,
        [next_up] + own_up[:-1] + [last] + swapped_up,
        [[base]] + arrived,
    )
    return finish(wide, total, swapped)


def solution(mesh):
    placed = (
        P(("group", "store"), "tensor"),
        P(("group", "store"), "tensor", None, None),
        P(("group", "store"), "tensor", None, None),
        P(("group", "store")),
        P("tensor", None),
        P("store", None, "tensor"),
        P("store", None, "tensor"),
        P(),
        P(),
        P(("group", "store"), None),
    )
    return jax.shard_map(
        functools.partial(shards, mesh),
        mesh=mesh,
        in_specs=placed,
        out_specs=P(("group", "store"), "tensor"),
        check_vma=False,
    )
```
